128 devices in a mesh: nodes: 16 (over x, z_hi, core), feat: 8 (over y, z_lo).
Axes of the slice: x: 4, y: 4, z: 4 (z_hi: 2, z_lo: 2; z = z_hi * 2 + z_lo), core: 2. Of those that a mesh axis runs over, the one named last changes fastest.
Arguments:
- feats: bfloat16 [128, 262144], P('feat', 'nodes'), may hold values from -6 to 6
- tile_src: int32 [2048, 20], P(('nodes', 'feat')), may hold values from 0 to 2047, as said below
- tile_weight: bfloat16 [2048, 20, 128, 128], P(('nodes', 'feat')), as said below
- w_one: bfloat16 [128, 512], replicated, may hold values from -0.5 to 0.5
- b_one: float32 [256], replicated, may hold values from -3 to 3
- w_two: bfloat16 [512, 256], replicated, may hold values from -0.375 to 0.375
- b_two: float32 [256], replicated, may hold values from -3 to 3
- cotangent: bfloat16 [262144, 256], P(('nodes', 'feat')), may hold values from -0.01171875 to 0.01171875
Outputs:
- layer_out: bfloat16 [262144, 256], P(('nodes', 'feat'))
- grad_w_two: float32 [512, 256], replicated
- grad_b_two: float32 [256], replicated
The draws below stay inside these ranges and needn't reach their ends.
Inputs may be any that keep to these rules, and one draw needn't show every extreme that they name: `tile_src`: the 20 source blocks of a block are distinct and lie among the blocks of its own device and of the devices just before and after it in node order, the last device followed by the first; a device holds 16 consecutive blocks. `tile_weight`: each destination node draws d neighbour samples, d from 15 to 25, with replacement among the 2560 source nodes of its block's tiles; each sample adds 1 / d (rounded to bfloat16 with its count) to that source's entry in the node's row, and all other entries are zero.
All inputs are finite; a program needn't handle non-finite values.
Results may differ from the reference program's by a relative error of at most 0.0048.
Values may be sent and summed in bfloat16 or wider, within the bound.
A program may use at most 128 MiB of HBM per device.

```python
import jax
import jax.numpy as jnp
from jax import lax

FEATS = 128
HIDDEN_SIZE = 256
TILE = 128
NEIGH = 20
FANOUT = 25
BDEV = 16
BLOCKS = 2048
NODES = 262144
DEVICES = 128


def draw_tile_src(key, part):
    key = jax.random.fold_in(key, 11)
    window = 3 * BDEV
    scores = jax.random.randint(key, (BLOCKS, window), 0, 1 << 20) * window + jnp.arange(window, dtype=jnp.int32)[None, :]
    order = jnp.argsort(scores, axis=1, stable=True)[:, :NEIGH].astype(jnp.int32)
    owner = (jnp.arange(BLOCKS, dtype=jnp.int32) // BDEV)[:, None]
    return ((owner - 1) * BDEV + order) % BLOCKS


def draw_tile_weight(key, part):
    key = jax.random.fold_in(key, 23)
    count_key, pick_key = jax.random.split(key)
    dest_rows = BLOCKS * TILE
    columns = NEIGH * TILE
    degree = jax.random.randint(count_key, (dest_rows,), FANOUT - 10, FANOUT + 1).astype(jnp.int32)
    picks = jax.random.randint(pick_key, (dest_rows, FANOUT), 0, columns).astype(jnp.int32)
    valid = (jnp.arange(FANOUT, dtype=jnp.int32)[None, :] < degree[:, None]).astype(jnp.int32)
    row_ids = jnp.broadcast_to(jnp.arange(dest_rows, dtype=jnp.int32)[:, None], (dest_rows, FANOUT))
    counts = jnp.zeros((dest_rows, columns), jnp.int32).at[row_ids, picks].add(valid)
    weights = counts.astype(jnp.float32) / degree.astype(jnp.float32)[:, None]
    weights = weights.reshape(BLOCKS, TILE, NEIGH, TILE).transpose(0, 2, 1, 3)
    return weights.astype(jnp.bfloat16)


def block_levels(rng, dims, cuts, least, largest):
    factor_of = 1.0
    for position, parts in cuts:
        draws = jax.random.uniform(jax.random.fold_in(jax.random.fold_in(rng, 6), position), (parts,), jnp.float32, least / len(cuts), largest / len(cuts))
        factor_of = factor_of * jnp.repeat(jnp.exp(draws), dims[position] // parts).reshape((-1,) + (1,) * (len(dims) - 1 - position))
    return factor_of


def noise(stream_key, extent, spread, reach, cuts=(), kind=jnp.bfloat16):
    loudness = block_levels(stream_key, extent, cuts, -0.22, 0.18) if cuts else 1.0
    values = jax.random.normal(stream_key, extent, jnp.float32) * spread * loudness
    return jnp.minimum(jnp.maximum(values, -reach), reach).astype(kind)


def setup_inputs(seed: int = 0) -> dict:
    key_list = jax.random.split(jax.random.key(seed), 9)
    return {
        "feats": noise(key_list[0], (FEATS, NODES), 1.0, 6.0, ((0, 8), (1, 16))),
        "tile_src": draw_tile_src(jax.random.fold_in(key_list[8], 71), 0),
        "tile_weight": draw_tile_weight(jax.random.fold_in(key_list[8], 71), 0),
        "w_one": noise(key_list[3], (FEATS, 2 * HIDDEN_SIZE), FEATS ** -0.5, 0.5),
        "b_one": noise(key_list[4], (HIDDEN_SIZE,), 0.5, 3.0, (), jnp.float32),
        "w_two": noise(key_list[5], (2 * HIDDEN_SIZE, HIDDEN_SIZE), HIDDEN_SIZE ** -0.5, 0.375),
        "b_two": noise(key_list[6], (HIDDEN_SIZE,), 0.5, 3.0, (), jnp.float32),
        "cotangent": noise(key_list[7], (NODES, HIDDEN_SIZE), (1.0 / (BDEV * TILE * DEVICES) ** 0.5), 0.01171875, ((0, 128),)),
    }


def aggregate(values, tile_src, tile_weight):
    width = values.shape[1]
    blocks = values.reshape(BLOCKS, TILE, width)

    def group(pair):
        sources, weights = pair
        picked = blocks[sources].astype(jnp.float32)
        return jnp.einsum("bkij,bkjc->bic", weights.astype(jnp.float32), picked)

    summed = lax.map(group, (tile_src.reshape(DEVICES, BDEV, NEIGH), tile_weight.reshape(DEVICES, BDEV, NEIGH, TILE, TILE)))
    return summed.reshape(NODES, width)


def reference(feats, tile_src, tile_weight, w_one, b_one, w_two, b_two, cotangent):
    proj = lax.dot_general(feats, w_one, (((0,), (0,)), ((), ())), preferred_element_type=jnp.float32)
    neigh_one = proj[:, HIDDEN_SIZE:].astype(jnp.bfloat16)
    hidden_one = jax.nn.relu(proj[:, :HIDDEN_SIZE] + aggregate(neigh_one, tile_src, tile_weight) + b_one).astype(jnp.bfloat16)
    mixed = aggregate(hidden_one, tile_src, tile_weight).astype(jnp.bfloat16)
    both = jnp.concatenate([hidden_one, mixed], axis=1)
    layer_out = (jnp.dot(both, w_two, preferred_element_type=jnp.float32) + b_two).astype(jnp.bfloat16)
    grad_w_two = lax.dot_general(both, cotangent, (((0,), (0,)), ((), ())), preferred_element_type=jnp.float32)
    grad_b_two = jnp.sum(cotangent.astype(jnp.float32), axis=0)
    return layer_out, grad_w_two, grad_b_two
```

```python
import functools

import jax
import jax.numpy as jnp
from jax import lax
from jax.experimental import pallas as pl
from jax.experimental.pallas import tpu as pltpu
from jax.sharding import PartitionSpec as P

BF = jnp.bfloat16
F32 = jnp.float32
TILE = 128
MESH = pl.DeviceIdType.MESH


def remote(src, dst, send_sem, recv_sem, node, feat):
    return pltpu.make_async_remote_copy(
        src_ref=src, dst_ref=dst, send_sem=send_sem, recv_sem=recv_sem,
        device_id=(node, feat), device_id_type=MESH)


def drain(ref, sem):
    pltpu.make_async_copy(ref, ref, sem).wait()


def dot(a, b):
    return lax.dot_general(a, b, (((1,), (0,)), ((), ())), preferred_element_type=F32)


def kernel(nn, nf, nb, neigh, chunk_blocks,
           feats, src, a_hbm, w1_hbm, b1, w2_hbm, b2, cot_hbm,
           out_hbm, gw_hbm, gb_out,
           ft, fn, a_v, pn, hn, mn, cot_v, cot_t, w1_v, w2_v, out_v,
           gt, rt, st, qt, ct, gb, rb, sb, qb, cb, gfin,
           load_sem, fsend, fedge, frecv, psend, pbound, pfsend, pdir, pfwd,
           ars, arr, out_sem):
    fd = feats.shape[0]
    rows = nb * TILE
    hid = b1.shape[1]
    rp = hid // nn
    hb = rp // 2
    ch = chunk_blocks
    nch = nb // ch
    cr = ch * TILE
    n = lax.axis_index("nodes")
    f = lax.axis_index("feat")
    z = lax.rem(f, 2)
    n_next = lax.rem(n + 1, nn)
    n_prev = lax.rem(n + nn - 1, nn)

    loads = [
        pltpu.make_async_copy(w1_hbm, w1_v, load_sem.at[0]),
        pltpu.make_async_copy(cot_hbm, cot_v, load_sem.at[1]),
        pltpu.make_async_copy(a_hbm, a_v, load_sem.at[2]),
        pltpu.make_async_copy(w2_hbm, w2_v, load_sem.at[3]),
    ]
    for load in loads:
        load.start()

    barrier = pltpu.get_barrier_semaphore()

    def greet(node, feat):
        pl.semaphore_signal(barrier, inc=1, device_id=(node, feat), device_id_type=MESH)

    for d in range(1, nf):
        greet(n, lax.rem(f + d, nf))
    for d in range(1, nn):
        greet(lax.rem(n + d, nn), f)

    @pl.when(f == 0)
    def _():
        for g in range(nf):
            greet(n_prev, jnp.int32(g))

    @pl.when(f == nf - 1)
    def _():
        for g in range(nf):
            greet(n_next, jnp.int32(g))

    pl.semaphore_wait(barrier, nf + nn)

    def feat_copy(part, d):
        df = lax.rem(f + d, nf)
        j = lax.rem(df + nf + part - 1, nf)
        if part == 0:
            dn = jnp.where(df == 0, n_next, n)
        elif part == 2:
            dn = jnp.where(df == nf - 1, n_prev, n)
        else:
            dn = n
        s = feats.at[:, pl.ds(pl.multiple_of(j * rows, rows), rows)]
        t = ft.at[pl.ds(pl.multiple_of(f * fd, fd), fd), pl.ds(part * rows, rows)]
        return s, t, dn, df

    for part in (1, 0, 2):
        for d in range(1, nf):
            s, t, dn, df = feat_copy(part, d)
            remote(s, t, fsend.at[part], frecv.at[part], dn, df).start()
        s, t, dn, df = feat_copy(part, 0)
        if part == 1:
            pltpu.make_async_copy(s, t, frecv.at[part]).start()
        else:
            edge = f == (0 if part == 0 else nf - 1)

            @pl.when(edge)
            def _():
                remote(s, t, fedge.at[part], frecv.at[part], dn, df).start()

            @pl.when(jnp.logical_not(edge))
            def _():
                pltpu.make_async_copy(s, t, frecv.at[part]).start()

    loads[1].wait()

    def cot_step(i, acc):
        base = pl.multiple_of(i * TILE, TILE)
        c = cot_v[pl.ds(base, TILE), :]
        cot_t[:, pl.ds(base, TILE)] = c.T
        return acc + c.astype(F32).reshape(TILE // hb, hb, hid).sum(0)

    bias_part = lax.fori_loop(0, nb, cot_step, jnp.zeros((hb, hid), F32))

    def turn(part):
        drain(ft.at[:, pl.ds(part * rows, rows)], frecv.at[part])

        def step(i, carry):
            base = pl.multiple_of(part * rows + i * TILE, TILE)
            fn[part * nb + i] = ft[:, pl.ds(base, TILE)].T
            return carry

        lax.fori_loop(0, nb, step, 0, unroll=2)

    turn(1)
    turn(0)
    turn(2)
    loads[0].wait()
    loads[2].wait()

    first = (n * nf + f - 1) * nb
    total = nn * nf * nb

    def gather(table, b):
        acc = None
        for k in range(0, neigh, 2):
            picked = []
            for i in (k, k + 1):
                s = src[b, i] - first
                s = jnp.where(s >= total, s - total, s)
                s = jnp.where(s < 0, s + total, s)
                s = jnp.minimum(s, 3 * nb - 1)
                picked.append(table[s])
            p = dot(jnp.concatenate([a_v[b, k], a_v[b, k + 1]], axis=1),
                    jnp.concatenate(picked, axis=0))
            acc = p if acc is None else acc + p
        return acc

    partner = f + 1 - 2 * z
    bound_next = jnp.logical_and(f == nf - 1, lax.rem(n, 2) == 1)
    bound_prev = jnp.logical_and(f == 0, lax.rem(n, 2) == 0)
    out_base = z * (2 * nb)
    in_base = (2 - 2 * z) * nb

    def at_rows(base, c):
        return pn.at[pl.ds(base + c * ch, ch)]

    def one_chunk(c, carry):
        for i in range(ch):
            b = c * ch + i
            pn[nb + b] = gather(fn, b).astype(BF)
        own = at_rows(nb, c)
        remote(own, at_rows(out_base, c), psend.at[c], pdir.at[c], n, partner).start()

        @pl.when(bound_next)
        def _():
            remote(own, at_rows(0, c), pbound.at[c], pfwd.at[c], n_next, jnp.int32(0)).start()

        @pl.when(bound_prev)
        def _():
            remote(own, at_rows(2 * nb, c), pbound.at[c], pfwd.at[c], n_prev, jnp.int32(nf - 1)).start()

        return carry

    lax.fori_loop(0, nch, one_chunk, 0)

    skip = jnp.logical_or(jnp.logical_and(f == nf - 2, lax.rem(n, 2) == 1),
                          jnp.logical_and(f == 1, lax.rem(n, 2) == 0))
    fwd_f = lax.rem(f + jnp.where(z == 0, 2, nf - 2), nf)
    fwd_n = jnp.where(f == nf - 2, n_next, jnp.where(f == 1, n_prev, n))

    def forward(c):
        drain(at_rows(in_base, c), pdir.at[c])

        @pl.when(jnp.logical_not(skip))
        def _():
            remote(at_rows(in_base, c), at_rows(out_base, c), pfsend.at[c], pfwd.at[c], fwd_n, fwd_f).start()

    w_cat = jnp.concatenate([w1_v[:, :hid], w1_v[:, hid:]], axis=0)
    bias_one = b1[...]

    def hidden(base, count):
        def step(i, carry):
            at = pl.ds(base + i * 2, 2)
            fp = jnp.concatenate([fn[at], pn[at]], axis=2).reshape(2 * TILE, 2 * TILE)
            v = dot(fp, w_cat) + bias_one
            hn[at] = jnp.maximum(v, 0.0).astype(BF).reshape(2, TILE, hid)
            return carry

        lax.fori_loop(0, count // 2, step, 0)

    def reduce_nodes(g, r, k):
        for d in range(1, nn):
            dn = lax.rem(n + d, nn)
            remote(g.at[dn], r.at[n], ars.at[k], arr.at[k], dn, f).start()
        r[n] = g[n]

    def reduce_feat(g, r, s, q, k):
        drain(r.at[pl.ds(0, nn - 1)], arr.at[k])
        drain(g.at[pl.ds(0, nn - 1)], ars.at[k])
        tot = r[0]
        for i in range(1, nn):
            tot = tot + r[i]
        for t in range(4):
            i, j = t // 2, t % 2
            s[t, :, 0:TILE] = tot[i * hb:(i + 1) * hb, j * TILE:(j + 1) * TILE]
            if s.shape[2] > TILE:
                s[t, :, TILE:] = tot[rp:, :]
        for d in range(1, nf):
            df = lax.rem(f + d, nf)
            remote(s.at[df // 2], q.at[f], ars.at[k + 1], arr.at[k + 1], n, df).start()
        q[f] = s[f // 2]

    def back_feat(s, q, c, k):
        drain(q.at[pl.ds(0, nf - 1)], arr.at[k + 1])
        drain(q.at[pl.ds(0, nf - 1)], ars.at[k + 1])
        tot = q[0]
        for i in range(1, nf):
            tot = tot + q[i]
        if q.shape[2] > TILE:
            gb_out[...] = jnp.sum(tot[:, TILE:], axis=0, keepdims=True)
        y = f // 2
        c[y] = tot[:, 0:TILE]
        for d in (2, 4, 6):
            remote(c.at[y], c.at[y], ars.at[k + 2], arr.at[k + 2], n, lax.rem(f + d, nf)).start()

    def back_nodes(c, half, k):
        drain(c.at[pl.ds(0, 3)], arr.at[k + 2])
        drain(c.at[pl.ds(0, 3)], ars.at[k + 2])
        at = pl.ds(pl.multiple_of(half * hid + n * rp, rp), rp)
        gfin[at, :] = jnp.concatenate(
            [jnp.concatenate([c[0], c[1]], axis=1), jnp.concatenate([c[2], c[3]], axis=1)], axis=0)
        for d in range(1, nn):
            remote(gfin.at[at], gfin.at[at], ars.at[k + 3], arr.at[k + 3], lax.rem(n + d, nn), f).start()

    def finish(half, k):
        some = gfin.at[pl.ds(half * hid, (nn - 1) * rp)]
        drain(some, arr.at[k + 3])
        drain(some, ars.at[k + 3])
        at = pl.ds(half * hid, hid)
        return pltpu.make_async_copy(gfin.at[at], gw_hbm.at[at], load_sem.at[4 + half])

    forward(0)
    hidden(nb, nb)
    if nch > 1:
        forward(1)
    g_top = dot(cot_t[...], hn[nb:2 * nb].reshape(rows, hid)).T
    for i in range(nn):
        gt[i, 0:rp, :] = g_top[i * rp:(i + 1) * rp, :]
        gt[i, rp:, :] = bias_part
    reduce_nodes(gt, rt, 0)
    for c in range(2, nch):
        forward(c)
    hidden(in_base, nb)
    reduce_feat(gt, rt, st, qt, 0)

    def halo(c):
        drain(at_rows(out_base, c), pfwd.at[c])
        hidden(out_base + c * ch, ch)

    halo(0)
    back_feat(st, qt, ct, 0)
    if nch > 1:
        halo(1)
    back_nodes(ct, 0, 0)
    for c in range(2, nch):
        halo(c)

    loads[3].wait()
    bias_two = b2[...]

    def two_chunk(c, carry):
        for i in range(ch):
            b = c * ch + i
            at = pl.ds(pl.multiple_of(b * TILE, TILE), TILE)
            mn[at, :] = gather(hn, b).astype(BF)
        at = pl.ds(pl.multiple_of(c * cr, cr), cr)
        own = hn[pl.ds(nb + c * ch, ch)].reshape(cr, hid)
        both = jnp.concatenate([own, mn[at, :]], axis=1)
        out_v[at, :] = (dot(both, w2_v[...]) + bias_two).astype(BF)
        pltpu.make_async_copy(out_v.at[at], out_hbm.at[at], out_sem.at[c]).start()
        return carry

    lax.fori_loop(0, nch, two_chunk, 0)

    g_bot = dot(cot_t[...], mn[...]).T
    for i in range(nn):
        gb[i] = g_bot[i * rp:(i + 1) * rp, :]
    reduce_nodes(gb, rb, 4)
    top = finish(0, 0)
    top.start()

    for part in range(3):
        drain(ft.at[pl.ds(0, (nf - 1) * fd), pl.ds(0, rows)], fsend.at[part])

    @pl.when(f == 0)
    def _():
        drain(ft.at[pl.ds(0, fd), pl.ds(0, rows)], fedge.at[0])

    @pl.when(f == nf - 1)
    def _():
        drain(ft.at[pl.ds(0, fd), pl.ds(0, rows)], fedge.at[2])

    for c in range(nch):
        drain(at_rows(nb, c), psend.at[c])

        @pl.when(jnp.logical_or(bound_next, bound_prev))
        def _():
            drain(at_rows(nb, c), pbound.at[c])

        @pl.when(jnp.logical_not(skip))
        def _():
            drain(at_rows(in_base, c), pfsend.at[c])

    reduce_feat(gb, rb, sb, qb, 4)
    back_feat(sb, qb, cb, 4)
    back_nodes(cb, 1, 4)
    for c in range(nch):
        drain(out_v.at[pl.ds(c * cr, cr)], out_sem.at[c])
    bottom = finish(1, 4)
    bottom.start()
    top.wait()
    bottom.wait()


def per_device(nn, nf, feats, tile_src, tile_weight, w_one, b_one, w_two, b_two, cotangent):
    fd = feats.shape[0]
    nb, neigh = tile_src.shape
    rows = nb * TILE
    hid = b_one.shape[0]
    features = w_one.shape[0]
    rp = hid // nn
    hb = rp // 2
    ch = min(4, nb)
    nch = nb // ch
    anyspace = pl.BlockSpec(memory_space=pl.ANY)
    vm = pl.BlockSpec(memory_space=pltpu.VMEM)
    sm = pl.BlockSpec(memory_space=pltpu.SMEM)
    dma = pltpu.SemaphoreType.DMA
    out, gw, gb = pl.pallas_call(
        functools.partial(kernel, nn, nf, nb, neigh, ch),
        out_shape=(
            jax.ShapeDtypeStruct((rows, hid), BF),
            jax.ShapeDtypeStruct((2 * hid, hid), F32),
            jax.ShapeDtypeStruct((1, hid), F32),
        ),
        in_specs=[anyspace, sm, anyspace, anyspace, vm, anyspace, vm, anyspace],
        out_specs=(anyspace, anyspace, vm),
        scratch_shapes=[
            pltpu.VMEM((features, 3 * rows), BF),
            pltpu.VMEM((3 * nb, TILE, features), BF),
            pltpu.VMEM(tile_weight.shape, BF),
            pltpu.VMEM((3 * nb, TILE, features), BF),
            pltpu.VMEM((3 * nb, TILE, hid), BF),
            pltpu.VMEM((rows, hid), BF),
            pltpu.VMEM((rows, hid), BF),
            pltpu.VMEM((hid, rows), BF),
            pltpu.VMEM(w_one.shape, BF),
            pltpu.VMEM(w_two.shape, BF),
            pltpu.VMEM((rows, hid), BF),
            pltpu.VMEM((nn, rp + hb, hid), F32),
            pltpu.VMEM((nn, rp + hb, hid), F32),
            pltpu.VMEM((4, hb, TILE + hid), F32),
            pltpu.VMEM((nf, hb, TILE + hid), F32),
            pltpu.VMEM((4, hb, TILE), F32),
            pltpu.VMEM((nn, rp, hid), F32),
            pltpu.VMEM((nn, rp, hid), F32),
            pltpu.VMEM((4, hb, TILE), F32),
            pltpu.VMEM((nf, hb, TILE), F32),
            pltpu.VMEM((4, hb, TILE), F32),
            pltpu.VMEM((2 * hid, hid), F32),
            dma((6,)), dma((3,)), dma((3,)), dma((3,)),
            dma((nch,)), dma((nch,)), dma((nch,)), dma((nch,)), dma((nch,)),
            dma((8,)), dma((8,)), dma((nch,)),
        ],
        compiler_params=pltpu.CompilerParams(
            collective_id=0, has_side_effects=True, vmem_limit_bytes=56 * 2**20),
        name="sage",
    )(feats, tile_src, tile_weight, w_one, b_one.reshape(1, hid), w_two, b_two.reshape(1, hid), cotangent)
    return out, gw, gb.reshape(hid)


def solution(mesh):
    nn, nf = mesh.shape["nodes"], mesh.shape["feat"]
    return jax.shard_map(
        functools.partial(per_device, nn, nf),
        mesh=mesh,
        in_specs=(
            P("feat", "nodes"),
            P(("nodes", "feat"), None),
            P(("nodes", "feat"), None, None, None),
            P(),
            P(),
            P(),
            P(),
            P(("nodes", "feat"), None),
        ),
        out_specs=(P(("nodes", "feat"), None), P(), P()),
        check_vma=False,
    )
```

```python
import functools

import jax
import jax.numpy as jnp
from jax import lax
from jax.experimental import pallas as pl
from jax.experimental.pallas import tpu as pltpu
from jax.sharding import PartitionSpec as P

BF = jnp.bfloat16
F32 = jnp.float32
TILE = 128
MESH = pl.DeviceIdType.MESH


def remote(src, dst, send_sem, recv_sem, node, feat):
    return pltpu.make_async_remote_copy(
        src_ref=src, dst_ref=dst, send_sem=send_sem, recv_sem=recv_sem,
        device_id=(node, feat), device_id_type=MESH)


def drain(ref, sem):
    pltpu.make_async_copy(ref, ref, sem).wait()


def dot(a, b):
    return lax.dot_general(a, b, (((1,), (0,)), ((), ())), preferred_element_type=F32)


def tiles_of(nn):
    tiles = max(nn // 2, 1)
    columns = min(tiles, 2)
    return tiles // columns, columns


def hand_over(a, b, c, x, y, z, sem):
    copies = [pltpu.make_async_copy(p, q, sem.at[i]) for i, (p, q) in enumerate(((a, x), (b, y), (c, z)))]
    for copy in copies:
        copy.start()
    for copy in copies:
        copy.wait()


def kernel(nn, nf, nb, neigh, chunk_blocks,
           feats, src, a_hbm, w1_hbm, b1, w2_hbm, b2, cot_hbm,
           out_hbm, gw_hbm, gb_out,
           ft, fn, a_v, pn, hn, mn, cot_v, cot_t, w1_v, w2_v, out_v,
           gt, rt, st, qt, ct, gb, rb, sb, qb, cb, gfin, gout, bslot,
           load_sem, fsend, fedge, frecv, psend, pbound, pfsend, pdir, pfwd,
           ars, arr, out_sem):
    fd = feats.shape[0]
    rows = nb * TILE
    hid = b1.shape[1]
    fp = hid // nf
    tr, tc = tiles_of(nn)
    th, tw = fp // tr, hid // tc
    ch = chunk_blocks
    nch = nb // ch
    cr = ch * TILE
    n = lax.axis_index("nodes")
    f = lax.axis_index("feat")
    z = lax.rem(f, 2)
    n_next = lax.rem(n + 1, nn)
    n_prev = lax.rem(n + nn - 1, nn)

    loads = [
        pltpu.make_async_copy(w1_hbm, w1_v, load_sem.at[0]),
        pltpu.make_async_copy(cot_hbm, cot_v, load_sem.at[1]),
        pltpu.make_async_copy(a_hbm, a_v, load_sem.at[2]),
        pltpu.make_async_copy(w2_hbm, w2_v, load_sem.at[3]),
    ]
    for load in loads:
        load.start()

    barrier = pltpu.get_barrier_semaphore()

    def greet(node, feat):
        pl.semaphore_signal(barrier, inc=1, device_id=(node, feat), device_id_type=MESH)

    for d in range(1, nf):
        greet(n, lax.rem(f + d, nf))
    for d in range(1, nn):
        greet(lax.rem(n + d, nn), f)

    @pl.when(f == 0)
    def _():
        for g in range(nf):
            greet(n_prev, jnp.int32(g))

    @pl.when(f == nf - 1)
    def _():
        for g in range(nf):
            greet(n_next, jnp.int32(g))

    pl.semaphore_wait(barrier, nf + nn)

    def feat_copy(part, d):
        df = lax.rem(f + d, nf)
        j = lax.rem(df + nf + part - 1, nf)
        if part == 0:
            dn = jnp.where(df == 0, n_next, n)
        elif part == 2:
            dn = jnp.where(df == nf - 1, n_prev, n)
        else:
            dn = n
        s = feats.at[:, pl.ds(pl.multiple_of(j * rows, rows), rows)]
        t = ft.at[pl.ds(pl.multiple_of(f * fd, fd), fd), pl.ds(part * rows, rows)]
        return s, t, dn, df

    for part in (1, 0, 2):
        for d in range(1, nf):
            s, t, dn, df = feat_copy(part, d)
            remote(s, t, fsend.at[part], frecv.at[part], dn, df).start()
        s, t, dn, df = feat_copy(part, 0)
        if part == 1:
            pltpu.make_async_copy(s, t, frecv.at[part]).start()
        else:
            edge = f == (0 if part == 0 else nf - 1)

            @pl.when(edge)
            def _():
                remote(s, t, fedge.at[part], frecv.at[part], dn, df).start()

            @pl.when(jnp.logical_not(edge))
            def _():
                pltpu.make_async_copy(s, t, frecv.at[part]).start()

    loads[1].wait()

    def cot_step(i, acc):
        base = pl.multiple_of(i * TILE, TILE)
        c = cot_v[pl.ds(base, TILE), :]
        cot_t[:, pl.ds(base, TILE)] = c.T
        return acc + c.astype(F32).reshape(TILE // th, th, hid).sum(0)

    bias_part = lax.fori_loop(0, nb, cot_step, jnp.zeros((th, hid), F32))

    def turn(part):
        drain(ft.at[:, pl.ds(part * rows, rows)], frecv.at[part])

        def step(i, carry):
            base = pl.multiple_of(part * rows + i * TILE, TILE)
            fn[part * nb + i] = ft[:, pl.ds(base, TILE)].T
            return carry

        lax.fori_loop(0, nb, step, 0, unroll=2)

    turn(1)
    turn(0)
    turn(2)
    loads[0].wait()
    loads[2].wait()

    first = (n * nf + f - 1) * nb
    total = nn * nf * nb

    def gather(table, b):
        acc = None
        for k in range(0, neigh, 2):
            picked = []
            for i in (k, k + 1):
                s = src[b, i] - first
                s = jnp.where(s >= total, s - total, s)
                s = jnp.where(s < 0, s + total, s)
                s = jnp.minimum(s, 3 * nb - 1)
                picked.append(table[s])
            p = dot(jnp.concatenate([a_v[b, k], a_v[b, k + 1]], axis=1),
                    jnp.concatenate(picked, axis=0))
            acc = p if acc is None else acc + p
        return acc

    partner = f + 1 - 2 * z
    bound_next = jnp.logical_and(f == nf - 1, lax.rem(n, 2) == 1)
    bound_prev = jnp.logical_and(f == 0, lax.rem(n, 2) == 0)
    out_base = z * (2 * nb)
    in_base = (2 - 2 * z) * nb

    def at_rows(base, c):
        return pn.at[pl.ds(base + c * ch, ch)]

    def one_chunk(c, carry):
        for i in range(ch):
            b = c * ch + i
            pn[nb + b] = gather(fn, b).astype(BF)
        own = at_rows(nb, c)
        remote(own, at_rows(out_base, c), psend.at[c], pdir.at[c], n, partner).start()

        @pl.when(bound_next)
        def _():
            remote(own, at_rows(0, c), pbound.at[c], pfwd.at[c], n_next, jnp.int32(0)).start()

        @pl.when(bound_prev)
        def _():
            remote(own, at_rows(2 * nb, c), pbound.at[c], pfwd.at[c], n_prev, jnp.int32(nf - 1)).start()

        return carry

    lax.fori_loop(0, nch, one_chunk, 0)

    skip = jnp.logical_or(jnp.logical_and(f == nf - 2, lax.rem(n, 2) == 1),
                          jnp.logical_and(f == 1, lax.rem(n, 2) == 0))
    fwd_f = lax.rem(f + jnp.where(z == 0, 2, nf - 2), nf)
    fwd_n = jnp.where(f == nf - 2, n_next, jnp.where(f == 1, n_prev, n))

    def forward(c):
        drain(at_rows(in_base, c), pdir.at[c])

        @pl.when(jnp.logical_not(skip))
        def _():
            remote(at_rows(in_base, c), at_rows(out_base, c), pfsend.at[c], pfwd.at[c], fwd_n, fwd_f).start()

    w_cat = jnp.concatenate([w1_v[:, :hid], w1_v[:, hid:]], axis=0)
    bias_one = b1[...]

    def hidden(base, count):
        def step(i, carry):
            at = pl.ds(base + i * 2, 2)
            fp = jnp.concatenate([fn[at], pn[at]], axis=2).reshape(2 * TILE, 2 * TILE)
            v = dot(fp, w_cat) + bias_one
            hn[at] = jnp.maximum(v, 0.0).astype(BF).reshape(2, TILE, hid)
            return carry

        lax.fori_loop(0, count // 2, step, 0)

    def load_pieces(g, grad):
        for i in range(nf):
            g[i] = grad[i * fp:(i + 1) * fp, :].astype(BF)

    def reduce_feat(g, r, k):
        for d in range(1, nf):
            df = lax.rem(f + d, nf)
            remote(g.at[df], r.at[f], ars.at[k], arr.at[k], n, df).start()
        r[f] = g[f]

    def reduce_nodes(g, r, s, q, k, extra):
        drain(r.at[pl.ds(0, nf - 1)], arr.at[k])
        drain(g.at[pl.ds(0, nf - 1)], ars.at[k])
        tot = r[0].astype(F32)
        for i in range(1, nf):
            tot = tot + r[i].astype(F32)
        for t in range(tr * tc):
            i, j = t // tc, t % tc
            s[t, :, 0:tw] = tot[i * th:(i + 1) * th, j * tw:(j + 1) * tw]
            if extra is not None:
                s[t, :, tw:] = extra
        for d in range(1, nn):
            dn = lax.rem(n + d, nn)
            remote(s.at[dn // 2], q.at[n], ars.at[k + 1], arr.at[k + 1], dn, f).start()
        q[n] = s[n // 2]

    def back_nodes(q, c, k):
        drain(q.at[pl.ds(0, nn - 1)], arr.at[k + 1])
        drain(q.at[pl.ds(0, nn - 1)], ars.at[k + 1])
        tot = q[0]
        for i in range(1, nn):
            tot = tot + q[i]
        if q.shape[2] > tw:
            bslot[f] = tot[:, tw:]
        c[n // 2] = tot[:, 0:tw]
        for d in range(2, nn, 2):
            remote(c.at[n // 2], c.at[n // 2], ars.at[k + 2], arr.at[k + 2], lax.rem(n + d, nn), f).start()

    def back_feat(c, half, k):
        if nn > 2:
            drain(c.at[pl.ds(0, nn // 2 - 1)], arr.at[k + 2])
            drain(c.at[pl.ds(0, nn // 2 - 1)], ars.at[k + 2])
        at = pl.ds(pl.multiple_of(half * hid + f * fp, fp), fp)
        gfin[at, :] = jnp.concatenate(
            [jnp.concatenate([c[i * tc + j] for j in range(tc)], axis=1) for i in range(tr)], axis=0).astype(BF)
        for d in range(1, nf):
            df = lax.rem(f + d, nf)
            remote(gfin.at[at], gfin.at[at], ars.at[k + 3], arr.at[k + 3], n, df).start()
            if half == 0:
                remote(bslot.at[f], bslot.at[f], ars.at[8], arr.at[8], n, df).start()

    def finish(half, k):
        some = gfin.at[pl.ds(half * hid, (nf - 1) * fp)]
        drain(some, arr.at[k + 3])
        drain(some, ars.at[k + 3])
        at = pl.ds(half * hid, hid)
        gout[at, :] = gfin[at, :].astype(F32)
        return pltpu.make_async_copy(gout.at[at], gw_hbm.at[at], load_sem.at[4 + half])

    forward(0)
    hidden(nb, nb)
    if nch > 1:
        forward(1)
    g_top = dot(cot_t[...], hn[nb:2 * nb].reshape(rows, hid)).T
    load_pieces(gt, g_top)
    reduce_feat(gt, rt, 0)
    for c in range(2, nch):
        forward(c)
    hidden(in_base, nb)
    reduce_nodes(gt, rt, st, qt, 0, bias_part)

    def halo(c):
        drain(at_rows(out_base, c), pfwd.at[c])
        hidden(out_base + c * ch, ch)

    halo(0)
    back_nodes(qt, ct, 0)
    if nch > 1:
        halo(1)
    back_feat(ct, 0, 0)
    for c in range(2, nch):
        halo(c)

    loads[3].wait()
    bias_two = b2[...]

    def two_chunk(c, carry):
        for i in range(ch):
            b = c * ch + i
            at = pl.ds(pl.multiple_of(b * TILE, TILE), TILE)
            mn[at, :] = gather(hn, b).astype(BF)
        at = pl.ds(pl.multiple_of(c * cr, cr), cr)
        own = hn[pl.ds(nb + c * ch, ch)].reshape(cr, hid)
        both = jnp.concatenate([own, mn[at, :]], axis=1)
        out_v[at, :] = (dot(both, w2_v[...]) + bias_two).astype(BF)
        pltpu.make_async_copy(out_v.at[at], out_hbm.at[at], out_sem.at[c]).start()
        return carry

    lax.fori_loop(0, nch, two_chunk, 0)

    g_bot = dot(cot_t[...], mn[...]).T
    load_pieces(gb, g_bot)
    reduce_feat(gb, rb, 4)
    top = finish(0, 0)
    top.start()
    drain(bslot.at[pl.ds(0, nf - 1)], arr.at[8])
    drain(bslot.at[pl.ds(0, nf - 1)], ars.at[8])
    col = bslot[0]
    for i in range(1, nf):
        col = col + bslot[i]
    gb_out[...] = jnp.sum(col, axis=0, keepdims=True)

    for part in range(3):
        drain(ft.at[pl.ds(0, (nf - 1) * fd), pl.ds(0, rows)], fsend.at[part])

    @pl.when(f == 0)
    def _():
        drain(ft.at[pl.ds(0, fd), pl.ds(0, rows)], fedge.at[0])

    @pl.when(f == nf - 1)
    def _():
        drain(ft.at[pl.ds(0, fd), pl.ds(0, rows)], fedge.at[2])

    for c in range(nch):
        drain(at_rows(nb, c), psend.at[c])

        @pl.when(jnp.logical_or(bound_next, bound_prev))
        def _():
            drain(at_rows(nb, c), pbound.at[c])

        @pl.when(jnp.logical_not(skip))
        def _():
            drain(at_rows(in_base, c), pfsend.at[c])

    reduce_nodes(gb, rb, sb, qb, 4, None)
    back_nodes(qb, cb, 4)
    back_feat(cb, 1, 4)
    for c in range(nch):
        drain(out_v.at[pl.ds(c * cr, cr)], out_sem.at[c])
    bottom = finish(1, 4)
    bottom.start()
    top.wait()
    bottom.wait()


def per_device(nn, nf, feats, tile_src, tile_weight, w_one, b_one, w_two, b_two, cotangent):
    fd = feats.shape[0]
    nb, neigh = tile_src.shape
    rows = nb * TILE
    hid = b_one.shape[0]
    features = w_one.shape[0]
    fp = hid // nf
    tr, tc = tiles_of(nn)
    th, tw = fp // tr, hid // tc
    ch = min(4, nb)
    nch = nb // ch
    anyspace = pl.BlockSpec(memory_space=pl.ANY)
    vm = pl.BlockSpec(memory_space=pltpu.VMEM)
    sm = pl.BlockSpec(memory_space=pltpu.SMEM)
    dma = pltpu.SemaphoreType.DMA
    out, gw, gb = pl.pallas_call(
        functools.partial(kernel, nn, nf, nb, neigh, ch),
        out_shape=(
            jax.ShapeDtypeStruct((rows, hid), BF),
            jax.ShapeDtypeStruct((2 * hid, hid), F32),
            jax.ShapeDtypeStruct((1, hid), F32),
        ),
        in_specs=[anyspace, sm, anyspace, anyspace, vm, anyspace, vm, anyspace],
        out_specs=(anyspace, anyspace, vm),
        scratch_shapes=[
            pltpu.VMEM((features, 3 * rows), BF),
            pltpu.VMEM((3 * nb, TILE, features), BF),
            pltpu.VMEM(tile_weight.shape, BF),
            pltpu.VMEM((3 * nb, TILE, features), BF),
            pltpu.VMEM((3 * nb, TILE, hid), BF),
            pltpu.VMEM((rows, hid), BF),
            pltpu.VMEM((rows, hid), BF),
            pltpu.VMEM((hid, rows), BF),
            pltpu.VMEM(w_one.shape, BF),
            pltpu.VMEM(w_two.shape, BF),
            pltpu.VMEM((rows, hid), BF),
            pltpu.VMEM((nf, fp, hid), BF),
            pltpu.VMEM((nf, fp, hid), BF),
            pltpu.VMEM((tr * tc, th, tw + hid), F32),
            pltpu.VMEM((nn, th, tw + hid), F32),
            pltpu.VMEM((tr * tc, th, tw), F32),
            pltpu.VMEM((nf, fp, hid), BF),
            pltpu.VMEM((nf, fp, hid), BF),
            pltpu.VMEM((tr * tc, th, tw), F32),
            pltpu.VMEM((nn, th, tw), F32),
            pltpu.VMEM((tr * tc, th, tw), F32),
            pltpu.VMEM((2 * hid, hid), BF),
            pltpu.VMEM((2 * hid, hid), F32),
            pltpu.VMEM((nf, th, hid), F32),
            dma((6,)), dma((3,)), dma((3,)), dma((3,)),
            dma((nch,)), dma((nch,)), dma((nch,)), dma((nch,)), dma((nch,)),
            dma((9,)), dma((9,)), dma((nch,)),
        ],
        compiler_params=pltpu.CompilerParams(
            collective_id=0, has_side_effects=True, vmem_limit_bytes=56 * 2**20),
        name="sage",
    )(feats, tile_src, tile_weight, w_one, b_one.reshape(1, hid), w_two, b_two.reshape(1, hid), cotangent)
    out, gw, gb = pl.pallas_call(
        hand_over,
        out_shape=tuple(jax.ShapeDtypeStruct(v.shape, v.dtype) for v in (out, gw, gb)),
        in_specs=[anyspace] * 3,
        out_specs=(anyspace,) * 3,
        scratch_shapes=[dma((3,))],
        name="hand_over",
    )(out, gw, gb)
    return out, gw, gb.reshape(hid)


def solution(mesh):
    nn, nf = mesh.shape["nodes"], mesh.shape["feat"]
    return jax.shard_map(
        functools.partial(per_device, nn, nf),
        mesh=mesh,
        in_specs=(
            P("feat", "nodes"),
            P(("nodes", "feat"), None),
            P(("nodes", "feat"), None, None, None),
            P(),
            P(),
            P(),
            P(),
            P(("nodes", "feat"), None),
        ),
        out_specs=(P(("nodes", "feat"), None), P(), P()),
        check_vma=False,
    )
```

```python
import functools

import jax
import jax.numpy as jnp
from jax import lax
from jax.experimental import pallas as pl
from jax.experimental.pallas import tpu as pltpu
from jax.sharding import PartitionSpec as P

BF = jnp.bfloat16
F32 = jnp.float32
TILE = 128
MESH = pl.DeviceIdType.MESH


def remote(src, dst, send_sem, recv_sem, node, feat):
    return pltpu.make_async_remote_copy(
        src_ref=src, dst_ref=dst, send_sem=send_sem, recv_sem=recv_sem,
        device_id=(node, feat), device_id_type=MESH)


def drain(ref, sem):
    pltpu.make_async_copy(ref, ref, sem).wait()


def dot(a, b):
    return lax.dot_general(a, b, (((1,), (0,)), ((), ())), preferred_element_type=F32)


def hand_over(out, gw, gb, out_copy, gw_wide, gb_sum):
    out_copy[...] = out[...]
    gw_wide[...] = gw[...].astype(F32)
    tot = gb[0]
    for i in range(1, gb.shape[0]):
        tot = tot + gb[i]
    gb_sum[...] = jnp.sum(tot, axis=0, keepdims=True)


def kernel(nn, nf, nb, neigh, chunk_blocks,
           feats, src, a_hbm, w1_hbm, b1, w2_hbm, b2, cot_hbm,
           out_hbm, gw_hbm, gb_hbm,
           ft, fn, a_v, pn, hn, mn, cot_v, cot_t, w1_v, w2_v, out_v,
           gt, rt, qt, gb, rb, qb, gfin, bslot,
           load_sem, fsend, fedge, frecv, psend, pbound, pfsend, pdir, pfwd,
           ars, arr, out_sem):
    fd = feats.shape[0]
    rows = nb * TILE
    hid = b1.shape[1]
    rp = hid // nn
    ch = chunk_blocks
    nch = nb // ch
    cr = ch * TILE
    n = lax.axis_index("nodes")
    f = lax.axis_index("feat")
    z = lax.rem(f, 2)
    n_next = lax.rem(n + 1, nn)
    n_prev = lax.rem(n + nn - 1, nn)

    loads = [
        pltpu.make_async_copy(w1_hbm, w1_v, load_sem.at[0]),
        pltpu.make_async_copy(cot_hbm, cot_v, load_sem.at[1]),
        pltpu.make_async_copy(a_hbm, a_v, load_sem.at[2]),
        pltpu.make_async_copy(w2_hbm, w2_v, load_sem.at[3]),
    ]
    for load in loads:
        load.start()

    barrier = pltpu.get_barrier_semaphore()

    def greet(node, feat):
        pl.semaphore_signal(barrier, inc=1, device_id=(node, feat), device_id_type=MESH)

    for d in range(1, nf):
        greet(n, lax.rem(f + d, nf))
    for d in range(1, nn):
        greet(lax.rem(n + d, nn), f)

    @pl.when(f == 0)
    def _():
        for g in range(nf):
            greet(n_prev, jnp.int32(g))

    @pl.when(f == nf - 1)
    def _():
        for g in range(nf):
            greet(n_next, jnp.int32(g))

    pl.semaphore_wait(barrier, nf + nn)

    def feat_copy(part, d):
        df = lax.rem(f + d, nf)
        j = lax.rem(df + nf + part - 1, nf)
        if part == 0:
            dn = jnp.where(df == 0, n_next, n)
        elif part == 2:
            dn = jnp.where(df == nf - 1, n_prev, n)
        else:
            dn = n
        s = feats.at[:, pl.ds(pl.multiple_of(j * rows, rows), rows)]
        t = ft.at[pl.ds(pl.multiple_of(f * fd, fd), fd), pl.ds(part * rows, rows)]
        return s, t, dn, df

    for part in (1, 0, 2):
        for d in range(1, nf):
            s, t, dn, df = feat_copy(part, d)
            remote(s, t, fsend.at[part], frecv.at[part], dn, df).start()
        s, t, dn, df = feat_copy(part, 0)
        if part == 1:
            pltpu.make_async_copy(s, t, frecv.at[part]).start()
        else:
            edge = f == (0 if part == 0 else nf - 1)

            @pl.when(edge)
            def _():
                remote(s, t, fedge.at[part], frecv.at[part], dn, df).start()

            @pl.when(jnp.logical_not(edge))
            def _():
                pltpu.make_async_copy(s, t, frecv.at[part]).start()

    loads[1].wait()

    def cot_step(i, acc):
        base = pl.multiple_of(i * TILE, TILE)
        c = cot_v[pl.ds(base, TILE), :]
        cot_t[:, pl.ds(base, TILE)] = c.T
        return acc + c.astype(F32).reshape(TILE // 8, 8, hid).sum(0)

    bias_part = lax.fori_loop(0, nb, cot_step, jnp.zeros((8, hid), F32))

    def turn(part):
        drain(ft.at[:, pl.ds(part * rows, rows)], frecv.at[part])

        def step(i, carry):
            base = pl.multiple_of(part * rows + i * TILE, TILE)
            fn[part * nb + i] = ft[:, pl.ds(base, TILE)].T
            return carry

        lax.fori_loop(0, nb, step, 0, unroll=2)

    turn(1)
    turn(0)
    turn(2)
    loads[0].wait()
    loads[2].wait()

    first = (n * nf + f - 1) * nb
    total = nn * nf * nb

    def gather(table, b):
        acc = None
        for k in range(0, neigh, 2):
            picked = []
            for i in (k, k + 1):
                s = src[b, i] - first
                s = jnp.where(s >= total, s - total, s)
                s = jnp.where(s < 0, s + total, s)
                s = jnp.minimum(s, 3 * nb - 1)
                picked.append(table[s])
            p = dot(jnp.concatenate([a_v[b, k], a_v[b, k + 1]], axis=1),
                    jnp.concatenate(picked, axis=0))
            acc = p if acc is None else acc + p
        return acc

    partner = f + 1 - 2 * z
    bound_next = jnp.logical_and(f == nf - 1, lax.rem(n, 2) == 1)
    bound_prev = jnp.logical_and(f == 0, lax.rem(n, 2) == 0)
    out_base = z * (2 * nb)
    in_base = (2 - 2 * z) * nb

    def at_rows(base, c):
        return pn.at[pl.ds(base + c * ch, ch)]

    def one_chunk(c, carry):
        for i in range(ch):
            b = c * ch + i
            pn[nb + b] = gather(fn, b).astype(BF)
        own = at_rows(nb, c)
        remote(own, at_rows(out_base, c), psend.at[c], pdir.at[c], n, partner).start()

        @pl.when(bound_next)
        def _():
            remote(own, at_rows(0, c), pbound.at[c], pfwd.at[c], n_next, jnp.int32(0)).start()

        @pl.when(bound_prev)
        def _():
            remote(own, at_rows(2 * nb, c), pbound.at[c], pfwd.at[c], n_prev, jnp.int32(nf - 1)).start()

        return carry

    lax.fori_loop(0, nch, one_chunk, 0)

    skip = jnp.logical_or(jnp.logical_and(f == nf - 2, lax.rem(n, 2) == 1),
                          jnp.logical_and(f == 1, lax.rem(n, 2) == 0))
    fwd_f = lax.rem(f + jnp.where(z == 0, 2, nf - 2), nf)
    fwd_n = jnp.where(f == nf - 2, n_next, jnp.where(f == 1, n_prev, n))

    def forward(c):
        drain(at_rows(in_base, c), pdir.at[c])

        @pl.when(jnp.logical_not(skip))
        def _():
            remote(at_rows(in_base, c), at_rows(out_base, c), pfsend.at[c], pfwd.at[c], fwd_n, fwd_f).start()

    w_cat = jnp.concatenate([w1_v[:, :hid], w1_v[:, hid:]], axis=0)
    bias_one = b1[...]

    def hidden(base, count):
        def step(i, carry):
            at = pl.ds(base + i * 2, 2)
            fp = jnp.concatenate([fn[at], pn[at]], axis=2).reshape(2 * TILE, 2 * TILE)
            v = dot(fp, w_cat) + bias_one
            hn[at] = jnp.maximum(v, 0.0).astype(BF).reshape(2, TILE, hid)
            return carry

        lax.fori_loop(0, count // 2, step, 0)

    def scatter_nodes(g, r, grad, k):
        for i in range(nn):
            g[i] = grad[i * rp:(i + 1) * rp, :].astype(BF)
        for d in range(1, nn):
            dn = lax.rem(n + d, nn)
            remote(g.at[dn], r.at[n], ars.at[k], arr.at[k], dn, f).start()
        r[n] = g[n]

    def share_feat(g, r, q, k, extra):
        drain(r.at[pl.ds(0, nn - 1)], arr.at[k])
        drain(g.at[pl.ds(0, nn - 1)], ars.at[k])
        tot = r[0].astype(F32)
        for i in range(1, nn):
            tot = tot + r[i].astype(F32)
        q[f, 0:rp, :] = tot
        if extra is not None:
            q[f, rp:, :] = extra
        for d in range(1, nf):
            remote(q.at[f], q.at[f], ars.at[k + 1], arr.at[k + 1], n, lax.rem(f + d, nf)).start()

    def gather_nodes(q, half, k):
        drain(q.at[pl.ds(0, nf - 1)], arr.at[k + 1])
        drain(q.at[pl.ds(0, nf - 1)], ars.at[k + 1])
        tot = q[0]
        for i in range(1, nf):
            tot = tot + q[i]
        at = pl.ds(pl.multiple_of(half * hid + n * rp, rp), rp)
        gfin[at, :] = tot[0:rp, :].astype(BF)
        for d in range(1, nn):
            remote(gfin.at[at], gfin.at[at], ars.at[k + 2], arr.at[k + 2], lax.rem(n + d, nn), f).start()
        if half == 0:
            bslot[n] = tot[rp:, :]
            for d in range(1, nn):
                remote(bslot.at[n], bslot.at[n], ars.at[6], arr.at[6], lax.rem(n + d, nn), f).start()

    def finish(half, k):
        some = gfin.at[pl.ds(half * hid, (nn - 1) * rp)]
        drain(some, arr.at[k + 2])
        drain(some, ars.at[k + 2])
        at = pl.ds(half * hid, hid)
        return pltpu.make_async_copy(gfin.at[at], gw_hbm.at[at], load_sem.at[4 + half])

    def halo(c):
        drain(at_rows(out_base, c), pfwd.at[c])
        hidden(out_base + c * ch, ch)

    hidden(nb, nb)
    scatter_nodes(gt, rt, dot(cot_t[...], hn[nb:2 * nb].reshape(rows, hid)).T, 0)
    for c in range(nch):
        forward(c)
        if c == min(1, nch - 1):
            share_feat(gt, rt, qt, 0, bias_part)
    hidden(in_base, nb)
    gather_nodes(qt, 0, 0)
    for c in range(nch):
        halo(c)

    loads[3].wait()
    bias_two = b2[...]

    def two_chunk(c, carry):
        for i in range(ch):
            b = c * ch + i
            at = pl.ds(pl.multiple_of(b * TILE, TILE), TILE)
            mn[at, :] = gather(hn, b).astype(BF)
        at = pl.ds(pl.multiple_of(c * cr, cr), cr)
        own = hn[pl.ds(nb + c * ch, ch)].reshape(cr, hid)
        both = jnp.concatenate([own, mn[at, :]], axis=1)
        out_v[at, :] = (dot(both, w2_v[...]) + bias_two).astype(BF)
        pltpu.make_async_copy(out_v.at[at], out_hbm.at[at], out_sem.at[c]).start()
        return carry

    lax.fori_loop(0, nch, two_chunk, 0)

    scatter_nodes(gb, rb, dot(cot_t[...], mn[...]).T, 3)
    top = finish(0, 0)
    top.start()
    drain(bslot.at[pl.ds(0, nn - 1)], arr.at[6])
    drain(bslot.at[pl.ds(0, nn - 1)], ars.at[6])
    bias = pltpu.make_async_copy(bslot, gb_hbm, load_sem.at[6])
    bias.start()

    for part in range(3):
        drain(ft.at[pl.ds(0, (nf - 1) * fd), pl.ds(0, rows)], fsend.at[part])

    @pl.when(f == 0)
    def _():
        drain(ft.at[pl.ds(0, fd), pl.ds(0, rows)], fedge.at[0])

    @pl.when(f == nf - 1)
    def _():
        drain(ft.at[pl.ds(0, fd), pl.ds(0, rows)], fedge.at[2])

    for c in range(nch):
        drain(at_rows(nb, c), psend.at[c])

        @pl.when(jnp.logical_or(bound_next, bound_prev))
        def _():
            drain(at_rows(nb, c), pbound.at[c])

        @pl.when(jnp.logical_not(skip))
        def _():
            drain(at_rows(in_base, c), pfsend.at[c])

    share_feat(gb, rb, qb, 3, None)
    gather_nodes(qb, 1, 3)
    for c in range(nch):
        drain(out_v.at[pl.ds(c * cr, cr)], out_sem.at[c])
    bottom = finish(1, 3)
    bottom.start()
    top.wait()
    bias.wait()
    bottom.wait()


def per_device(nn, nf, feats, tile_src, tile_weight, w_one, b_one, w_two, b_two, cotangent):
    fd = feats.shape[0]
    nb, neigh = tile_src.shape
    rows = nb * TILE
    hid = b_one.shape[0]
    features = w_one.shape[0]
    rp = hid // nn
    ch = min(4, nb)
    nch = nb // ch
    anyspace = pl.BlockSpec(memory_space=pl.ANY)
    vm = pl.BlockSpec(memory_space=pltpu.VMEM)
    sm = pl.BlockSpec(memory_space=pltpu.SMEM)
    dma = pltpu.SemaphoreType.DMA
    out, gw, gb = pl.pallas_call(
        functools.partial(kernel, nn, nf, nb, neigh, ch),
        out_shape=(
            jax.ShapeDtypeStruct((rows, hid), BF),
            jax.ShapeDtypeStruct((2 * hid, hid), BF),
            jax.ShapeDtypeStruct((nn, 8, hid), F32),
        ),
        in_specs=[anyspace, sm, anyspace, anyspace, vm, anyspace, vm, anyspace],
        out_specs=(anyspace,) * 3,
        scratch_shapes=[
            pltpu.VMEM((features, 3 * rows), BF),
            pltpu.VMEM((3 * nb, TILE, features), BF),
            pltpu.VMEM(tile_weight.shape, BF),
            pltpu.VMEM((3 * nb, TILE, features), BF),
            pltpu.VMEM((3 * nb, TILE, hid), BF),
            pltpu.VMEM((rows, hid), BF),
            pltpu.VMEM((rows, hid), BF),
            pltpu.VMEM((hid, rows), BF),
            pltpu.VMEM(w_one.shape, BF),
            pltpu.VMEM(w_two.shape, BF),
            pltpu.VMEM((rows, hid), BF),
            pltpu.VMEM((nn, rp, hid), BF),
            pltpu.VMEM((nn, rp, hid), BF),
            pltpu.VMEM((nf, rp + 8, hid), F32),
            pltpu.VMEM((nn, rp, hid), BF),
            pltpu.VMEM((nn, rp, hid), BF),
            pltpu.VMEM((nf, rp, hid), F32),
            pltpu.VMEM((2 * hid, hid), BF),
            pltpu.VMEM((nn, 8, hid), F32),
            dma((7,)), dma((3,)), dma((3,)), dma((3,)),
            dma((nch,)), dma((nch,)), dma((nch,)), dma((nch,)), dma((nch,)),
            dma((7,)), dma((7,)), dma((nch,)),
        ],
        compiler_params=pltpu.CompilerParams(
            collective_id=0, has_side_effects=True, vmem_limit_bytes=56 * 2**20),
        name="sage",
    )(feats, tile_src, tile_weight, w_one, b_one.reshape(1, hid), w_two, b_two.reshape(1, hid), cotangent)
    out, gw, gb = pl.pallas_call(
        hand_over,
        out_shape=(
            jax.ShapeDtypeStruct((rows, hid), BF),
            jax.ShapeDtypeStruct((2 * hid, hid), F32),
            jax.ShapeDtypeStruct((1, hid), F32),
        ),
        in_specs=[vm] * 3,
        out_specs=(vm,) * 3,
        name="hand_over",
    )(out, gw, gb)
    return out, gw, gb.reshape(hid)


def solution(mesh):
    nn, nf = mesh.shape["nodes"], mesh.shape["feat"]
    return jax.shard_map(
        functools.partial(per_device, nn, nf),
        mesh=mesh,
        in_specs=(
            P("feat", "nodes"),
            P(("nodes", "feat"), None),
            P(("nodes", "feat"), None, None, None),
            P(),
            P(),
            P(),
            P(),
            P(("nodes", "feat"), None),
        ),
        out_specs=(P(("nodes", "feat"), None), P(), P()),
        check_vma=False,
    )
```

```python
import functools

import jax
import jax.numpy as jnp
from jax import lax
from jax.experimental import pallas as pl
from jax.experimental.pallas import tpu as pltpu
from jax.sharding import PartitionSpec as P

BF = jnp.bfloat16
F32 = jnp.float32
TILE = 128
MESH = pl.DeviceIdType.MESH


def remote(src, dst, send_sem, recv_sem, node, feat):
    return pltpu.make_async_remote_copy(
        src_ref=src, dst_ref=dst, send_sem=send_sem, recv_sem=recv_sem,
        device_id=(node, feat), device_id_type=MESH)


def drain(ref, sem):
    pltpu.make_async_copy(ref, ref, sem).wait()


def dot(a, b):
    return lax.dot_general(a, b, (((1,), (0,)), ((), ())), preferred_element_type=F32)


def dot_nt(a, b):
    return lax.dot_general(a, b, (((1,), (1,)), ((), ())), preferred_element_type=F32)


def hand_over(out, gw, gb, out_copy, gw_wide, gb_sum):
    out_copy[...] = out[...]
    gw_wide[...] = gw[...].astype(F32)
    tot = gb[0]
    for i in range(1, gb.shape[0]):
        tot = tot + gb[i]
    gb_sum[...] = jnp.sum(tot, axis=0, keepdims=True)


def kernel(nn, nf, nb, neigh, chunk_blocks,
           feats, src, a_hbm, w1_hbm, b1, w2_hbm, b2, cot_hbm,
           out_hbm, gw_hbm, gb_hbm,
           ft, zb, fa, fb, a_v, pt, hn, mn, cot_v, cot_t, w1_v, w2_v, out_v,
           gt, rt, qt, gb, rb, qb, gfin, bslot,
           load_sem, zsend, zrecv, fsend, fedge, frecv, psend, pbound, pfsend, pdir, pfwd,
           ars, arr, out_sem):
    fd = feats.shape[0]
    rows = nb * TILE
    hid = b1.shape[1]
    rp = hid // nn
    ch = chunk_blocks
    nch = nb // ch
    cr = ch * TILE
    n = lax.axis_index("nodes")
    f = lax.axis_index("feat")
    z = lax.rem(f, 2)
    n_next = lax.rem(n + 1, nn)
    n_prev = lax.rem(n + nn - 1, nn)

    loads = [
        pltpu.make_async_copy(w1_hbm, w1_v, load_sem.at[0]),
        pltpu.make_async_copy(cot_hbm, cot_v, load_sem.at[1]),
        pltpu.make_async_copy(a_hbm, a_v, load_sem.at[2]),
        pltpu.make_async_copy(w2_hbm, w2_v, load_sem.at[3]),
    ]
    for load in loads:
        load.start()

    barrier = pltpu.get_barrier_semaphore()

    def greet(node, feat):
        pl.semaphore_signal(barrier, inc=1, device_id=(node, feat), device_id_type=MESH)

    for d in range(1, nf):
        greet(n, lax.rem(f + d, nf))
    for d in range(1, nn):
        greet(lax.rem(n + d, nn), f)

    @pl.when(f == 0)
    def _():
        for g in range(nf):
            greet(n_prev, jnp.int32(g))

    @pl.when(f == nf - 1)
    def _():
        for g in range(nf):
            greet(n_next, jnp.int32(g))

    pl.semaphore_wait(barrier, nf + nn)

    partner = f + 1 - 2 * z
    half = nf * fd // 2
    row_own = (f // 2) * fd + z * half
    row_other = (f // 2) * fd + (1 - z) * half

    def columns(j):
        return pl.ds(pl.multiple_of(j * rows, rows), rows)

    for t in range(nf):
        j = lax.rem(partner + t, nf)
        remote(feats.at[:, columns(j)], zb.at[:, columns(j)], zsend.at[0], zrecv.at[t], n, partner).start()

    def spread(t, source, row, h):
        j = lax.rem(f + t, nf)
        s = source.at[:, columns(j)]

        def to(part):
            return ft.at[pl.ds(pl.multiple_of(row, fd), fd), pl.ds(part * rows, rows)]

        def keep(part):
            pltpu.make_async_copy(s, to(part), frecv.at[h]).start()

        if t % 2 == 0:
            if t == 0:
                keep(1)
            else:
                remote(s, to(1), fsend.at[h], frecv.at[h], n, j).start()
            return
        dn = jnp.where(j == nf - 1, n_next, n)
        df = lax.rem(j + 1, nf)
        if t == nf - 1:
            @pl.when(f == 0)
            def _():
                remote(s, to(0), fedge.at[h], frecv.at[h], dn, df).start()

            @pl.when(f != 0)
            def _():
                keep(0)
        else:
            remote(s, to(0), fsend.at[h], frecv.at[h], dn, df).start()
        dn = jnp.where(j == 0, n_prev, n)
        df = lax.rem(j + nf - 1, nf)
        if t == 1:
            @pl.when(f == nf - 1)
            def _():
                remote(s, to(2), fedge.at[h], frecv.at[h], dn, df).start()

            @pl.when(f != nf - 1)
            def _():
                keep(2)
        else:
            remote(s, to(2), fsend.at[h], frecv.at[h], dn, df).start()

    for t in range(nf):
        spread(t, feats, row_own, 0)

    def pass_on(t):
        drain(zb.at[:, pl.ds(0, rows)], zrecv.at[t])
        spread(t, zb, row_other, 1)

    loads[1].wait()

    def cot_step(i, acc):
        base = pl.multiple_of(i * TILE, TILE)
        c = cot_v[pl.ds(base, TILE), :]
        cot_t[:, pl.ds(base, TILE)] = c.T
        return acc + c.astype(F32).reshape(TILE // 8, 8, hid).sum(0)

    bias_part = lax.fori_loop(0, nb // 2, cot_step, jnp.zeros((8, hid), F32))
    pass_on(0)
    bias_part = lax.fori_loop(nb // 2, nb, cot_step, bias_part)
    for t in range(1, nf - 2):
        pass_on(t)

    first = (n * nf + f - 1) * nb
    total = nn * nf * nb

    def pick(table, b, k):
        s = src[b, k] - first
        s = jnp.where(s >= total, s - total, s)
        s = jnp.where(s < 0, s + total, s)
        return table[jnp.minimum(s, 3 * nb - 1)]

    def pair(b, k):
        return jnp.concatenate([a_v[b, k], a_v[b, k + 1]], axis=1)

    bound_next = jnp.logical_and(f == nf - 1, lax.rem(n, 2) == 1)
    bound_prev = jnp.logical_and(f == 0, lax.rem(n, 2) == 0)
    out_base = z * (2 * nb)
    in_base = (2 - 2 * z) * nb

    def at_cols(row, base, c):
        return pt.at[pl.ds(pl.multiple_of(row, half), half),
                     pl.ds(pl.multiple_of((base + c * ch) * TILE, cr), cr)]

    def arrange(table, row, h):
        drain(ft.at[pl.ds(0, half)], frecv.at[h])

        def step(i, carry):
            table[i] = ft[pl.ds(pl.multiple_of(row, half), half), pl.ds(pl.multiple_of(i * TILE, TILE), TILE)]
            return carry

        lax.fori_loop(0, 3 * nb, step, 0, unroll=4)

    def one_chunk(table, row, h, c):
        for i in range(ch):
            b = c * ch + i
            acc = None
            for k in range(0, neigh, 2):
                p = dot_nt(jnp.concatenate([pick(table, b, k), pick(table, b, k + 1)], axis=1), pair(b, k))
                acc = p if acc is None else acc + p
            pt[pl.ds(pl.multiple_of(row, half), half),
               pl.ds(pl.multiple_of((nb + b) * TILE, TILE), TILE)] = acc.astype(BF)
        m = h * nch + c
        own = at_cols(row, nb, c)
        remote(own, at_cols(row, out_base, c), psend.at[m], pdir.at[m], n, partner).start()

        @pl.when(bound_next)
        def _():
            remote(own, at_cols(row, 0, c), pbound.at[m], pfwd.at[m], n_next, jnp.int32(0)).start()

        @pl.when(bound_prev)
        def _():
            remote(own, at_cols(row, 2 * nb, c), pbound.at[m], pfwd.at[m], n_prev, jnp.int32(nf - 1)).start()

    skip = jnp.logical_or(jnp.logical_and(f == nf - 2, lax.rem(n, 2) == 1),
                          jnp.logical_and(f == 1, lax.rem(n, 2) == 0))
    fwd_f = lax.rem(f + jnp.where(z == 0, 2, nf - 2), nf)
    fwd_n = jnp.where(f == nf - 2, n_next, jnp.where(f == 1, n_prev, n))

    def forward(h, c):
        m = h * nch + c
        row = (1 - z) * half if h == 0 else z * half
        came = at_cols(row, in_base, c)
        drain(came, pdir.at[m])

        @pl.when(jnp.logical_not(skip))
        def _():
            remote(came, at_cols(row, out_base, c), pfsend.at[m], pfwd.at[m], fwd_n, fwd_f).start()

    arrange(fa, z * half, 0)
    loads[2].wait()
    one_chunk(fa, z * half, 0, 0)
    pass_on(nf - 2)
    if nch > 1:
        one_chunk(fa, z * half, 0, 1)
    pass_on(nf - 1)
    if nch > 2:
        lax.fori_loop(2, nch, lambda c, u: (one_chunk(fa, z * half, 0, c), u)[1], 0)
    arrange(fb, (1 - z) * half, 1)

    def second(c, carry):
        one_chunk(fb, (1 - z) * half, 1, c)
        forward(0, c)
        return carry

    lax.fori_loop(0, nch, second, 0)

    loads[0].wait()
    order = [g * fd for g in range(0, nf, 2)] + [g * fd for g in range(1, nf, 2)]
    w_cat = jnp.concatenate(
        [w1_v[g:g + fd, :hid] for g in order] + [w1_v[g:g + fd, hid:] for g in order], axis=0)
    bias_one = b1[...]

    def hidden(base, count):
        def step(i, carry):
            at = pl.ds(base + i * 2, 2)
            cols = pl.ds(pl.multiple_of((base + i * 2) * TILE, 2 * TILE), 2 * TILE)
            v = dot(jnp.concatenate([ft[:, cols], pt[:, cols]], axis=0).T, w_cat) + bias_one
            hn[at] = jnp.maximum(v, 0.0).astype(BF).reshape(2, TILE, hid)
            return carry

        lax.fori_loop(0, count // 2, step, 0)

    def scatter_nodes(g, r, grad, k):
        for i in range(nn):
            g[i] = grad[i * rp:(i + 1) * rp, :].astype(BF)
        for d in range(1, nn):
            dn = lax.rem(n + d, nn)
            remote(g.at[dn], r.at[n], ars.at[k], arr.at[k], dn, f).start()
        r[n] = g[n]

    def share_feat(g, r, q, k, extra):
        drain(r.at[pl.ds(0, nn - 1)], arr.at[k])
        drain(g.at[pl.ds(0, nn - 1)], ars.at[k])
        tot = r[0].astype(F32)
        for i in range(1, nn):
            tot = tot + r[i].astype(F32)
        q[f, 0:rp, :] = tot
        if extra is not None:
            q[f, rp:, :] = extra
        for d in range(1, nf):
            remote(q.at[f], q.at[f], ars.at[k + 1], arr.at[k + 1], n, lax.rem(f + d, nf)).start()

    def gather_nodes(q, half, k):
        drain(q.at[pl.ds(0, nf - 1)], arr.at[k + 1])
        drain(q.at[pl.ds(0, nf - 1)], ars.at[k + 1])
        tot = q[0]
        for i in range(1, nf):
            tot = tot + q[i]
        at = pl.ds(pl.multiple_of(half * hid + n * rp, rp), rp)
        gfin[at, :] = tot[0:rp, :].astype(BF)
        for d in range(1, nn):
            remote(gfin.at[at], gfin.at[at], ars.at[k + 2], arr.at[k + 2], lax.rem(n + d, nn), f).start()
        if half == 0:
            bslot[n] = tot[rp:, :]
            for d in range(1, nn):
                remote(bslot.at[n], bslot.at[n], ars.at[6], arr.at[6], lax.rem(n + d, nn), f).start()

    def finish(half, k):
        some = gfin.at[pl.ds(half * hid, (nn - 1) * rp)]
        drain(some, arr.at[k + 2])
        drain(some, ars.at[k + 2])
        at = pl.ds(half * hid, hid)
        return pltpu.make_async_copy(gfin.at[at], gw_hbm.at[at], load_sem.at[4 + half])

    def halo(c):
        for h in range(2):
            drain(at_cols(0, out_base, c), pfwd.at[h * nch + c])
        hidden(out_base + c * ch, ch)

    hidden(nb, nb)
    scatter_nodes(gt, rt, dot(cot_t[...], hn[nb:2 * nb].reshape(rows, hid)).T, 0)
    for c in range(nch):
        forward(1, c)
        if c == min(1, nch - 1):
            share_feat(gt, rt, qt, 0, bias_part)
    hidden(in_base, nb)
    gather_nodes(qt, 0, 0)
    for c in range(nch):
        halo(c)

    loads[3].wait()
    bias_two = b2[...]

    def two_chunk(c, carry):
        for i in range(ch):
            b = c * ch + i
            at = pl.ds(pl.multiple_of(b * TILE, TILE), TILE)
            acc = None
            for k in range(0, neigh, 2):
                p = dot(pair(b, k), jnp.concatenate([pick(hn, b, k), pick(hn, b, k + 1)], axis=0))
                acc = p if acc is None else acc + p
            mn[at, :] = acc.astype(BF)
        at = pl.ds(pl.multiple_of(c * cr, cr), cr)
        own = hn[pl.ds(nb + c * ch, ch)].reshape(cr, hid)
        both = jnp.concatenate([own, mn[at, :]], axis=1)
        out_v[at, :] = (dot(both, w2_v[...]) + bias_two).astype(BF)
        pltpu.make_async_copy(out_v.at[at], out_hbm.at[at], out_sem.at[c]).start()
        return carry

    lax.fori_loop(0, nch, two_chunk, 0)

    scatter_nodes(gb, rb, dot(cot_t[...], mn[...]).T, 3)
    top = finish(0, 0)
    top.start()
    drain(bslot.at[pl.ds(0, nn - 1)], arr.at[6])
    drain(bslot.at[pl.ds(0, nn - 1)], ars.at[6])
    bias = pltpu.make_async_copy(bslot, gb_hbm, load_sem.at[6])
    bias.start()

    drain(zb, zsend.at[0])
    for h in range(2):
        drain(ft.at[pl.ds(0, (nf + 1) * fd // 3), :], fsend.at[h])

        @pl.when(jnp.logical_or(f == 0, f == nf - 1))
        def _():
            drain(ft.at[pl.ds(0, fd), pl.ds(0, rows)], fedge.at[h])

    for m in range(2 * nch):
        some = at_cols(0, 0, 0)
        drain(some, psend.at[m])

        @pl.when(jnp.logical_or(bound_next, bound_prev))
        def _():
            drain(some, pbound.at[m])

        @pl.when(jnp.logical_not(skip))
        def _():
            drain(some, pfsend.at[m])

    share_feat(gb, rb, qb, 3, None)
    gather_nodes(qb, 1, 3)
    for c in range(nch):
        drain(out_v.at[pl.ds(c * cr, cr)], out_sem.at[c])
    bottom = finish(1, 3)
    bottom.start()
    top.wait()
    bias.wait()
    bottom.wait()


def per_device(nn, nf, feats, tile_src, tile_weight, w_one, b_one, w_two, b_two, cotangent):
    fd = feats.shape[0]
    nb, neigh = tile_src.shape
    rows = nb * TILE
    hid = b_one.shape[0]
    features = w_one.shape[0]
    rp = hid // nn
    ch = min(4, nb)
    nch = nb // ch
    anyspace = pl.BlockSpec(memory_space=pl.ANY)
    vm = pl.BlockSpec(memory_space=pltpu.VMEM)
    sm = pl.BlockSpec(memory_space=pltpu.SMEM)
    dma = pltpu.SemaphoreType.DMA
    out, gw, gb = pl.pallas_call(
        functools.partial(kernel, nn, nf, nb, neigh, ch),
        out_shape=(
            jax.ShapeDtypeStruct((rows, hid), BF),
            jax.ShapeDtypeStruct((2 * hid, hid), BF),
            jax.ShapeDtypeStruct((nn, 8, hid), F32),
        ),
        in_specs=[anyspace, sm, anyspace, anyspace, vm, anyspace, vm, anyspace],
        out_specs=(anyspace,) * 3,
        scratch_shapes=[
            pltpu.VMEM((features, 3 * rows), BF),
            pltpu.VMEM((fd, nf * rows), BF),
            pltpu.VMEM((3 * nb, features // 2, TILE), BF),
            pltpu.VMEM((3 * nb, features // 2, TILE), BF),
            pltpu.VMEM(tile_weight.shape, BF),
            pltpu.VMEM((features, 3 * rows), BF),
            pltpu.VMEM((3 * nb, TILE, hid), BF),
            pltpu.VMEM((rows, hid), BF),
            pltpu.VMEM((rows, hid), BF),
            pltpu.VMEM((hid, rows), BF),
            pltpu.VMEM(w_one.shape, BF),
            pltpu.VMEM(w_two.shape, BF),
            pltpu.VMEM((rows, hid), BF),
            pltpu.VMEM((nn, rp, hid), BF),
            pltpu.VMEM((nn, rp, hid), BF),
            pltpu.VMEM((nf, rp + 8, hid), F32),
            pltpu.VMEM((nn, rp, hid), BF),
            pltpu.VMEM((nn, rp, hid), BF),
            pltpu.VMEM((nf, rp, hid), F32),
            pltpu.VMEM((2 * hid, hid), BF),
            pltpu.VMEM((nn, 8, hid), F32),
            dma((7,)), dma((1,)), dma((nf,)), dma((2,)), dma((2,)), dma((2,)),
            dma((2 * nch,)), dma((2 * nch,)), dma((2 * nch,)), dma((2 * nch,)), dma((2 * nch,)),
            dma((7,)), dma((7,)), dma((nch,)),
        ],
        compiler_params=pltpu.CompilerParams(
            collective_id=0, has_side_effects=True, vmem_limit_bytes=56 * 2**20),
        name="sage",
    )(feats, tile_src, tile_weight, w_one, b_one.reshape(1, hid), w_two, b_two.reshape(1, hid), cotangent)
    out, gw, gb = pl.pallas_call(
        hand_over,
        out_shape=(
            jax.ShapeDtypeStruct((rows, hid), BF),
            jax.ShapeDtypeStruct((2 * hid, hid), F32),
            jax.ShapeDtypeStruct((1, hid), F32),
        ),
        in_specs=[vm] * 3,
        out_specs=(vm,) * 3,
        name="hand_over",
    )(out, gw, gb)
    return out, gw, gb.reshape(hid)


def solution(mesh):
    nn, nf = mesh.shape["nodes"], mesh.shape["feat"]
    return jax.shard_map(
        functools.partial(per_device, nn, nf),
        mesh=mesh,
        in_specs=(
            P("feat", "nodes"),
            P(("nodes", "feat"), None),
            P(("nodes", "feat"), None, None, None),
            P(),
            P(),
            P(),
            P(),
            P(("nodes", "feat"), None),
        ),
        out_specs=(P(("nodes", "feat"), None), P(), P()),
        check_vma=False,
    )
```

```python
import functools

import jax
import jax.numpy as jnp
from jax import lax
from jax.experimental import pallas as pl
from jax.experimental.pallas import tpu as pltpu
from jax.sharding import PartitionSpec as P

BF = jnp.bfloat16
F32 = jnp.float32
TILE = 128
MESH = pl.DeviceIdType.MESH


def remote(src, dst, send_sem, recv_sem, node, feat):
    return pltpu.make_async_remote_copy(
        src_ref=src, dst_ref=dst, send_sem=send_sem, recv_sem=recv_sem,
        device_id=(node, feat), device_id_type=MESH)


def drain(ref, sem):
    pltpu.make_async_copy(ref, ref, sem).wait()


def dot(a, b):
    return lax.dot_general(a, b, (((1,), (0,)), ((), ())), preferred_element_type=F32)


def dot_nt(a, b):
    return lax.dot_general(a, b, (((1,), (1,)), ((), ())), preferred_element_type=F32)


def hand_over(out, gw, gb, out_copy, gw_wide, gb_sum):
    out_copy[...] = out[...]
    gw_wide[...] = gw[...].astype(F32)
    tot = gb[0]
    for i in range(1, gb.shape[0]):
        tot = tot + gb[i]
    gb_sum[...] = jnp.sum(tot, axis=0, keepdims=True)


def kernel(nn, nf, nb, neigh, chunk_blocks,
           feats, src, a_hbm, w1_hbm, b1, w2_hbm, b2, cot_hbm,
           out_hbm, gw_hbm, gb_hbm,
           ft, zb, fa, fb, a_v, pt, hn, mn, cot_v, cot_t, w1_v, w2_v, out_v,
           gt, rt, qt, gb, rb, qb, gfin, bslot,
           load_sem, zsend, zrecv, fsend, fedge, frecv, psend, pbound, pfsend, pdir, pfwd,
           ars, arr, out_sem):
    fd = feats.shape[0]
    rows = nb * TILE
    hid = b1.shape[1]
    rp = hid // nn
    ch = chunk_blocks
    nch = nb // ch
    cr = ch * TILE
    n = lax.axis_index("nodes")
    f = lax.axis_index("feat")
    z = lax.rem(f, 2)
    n_next = lax.rem(n + 1, nn)
    n_prev = lax.rem(n + nn - 1, nn)

    loads = [
        pltpu.make_async_copy(w1_hbm, w1_v, load_sem.at[0]),
        pltpu.make_async_copy(cot_hbm, cot_v, load_sem.at[1]),
        pltpu.make_async_copy(a_hbm, a_v, load_sem.at[2]),
        pltpu.make_async_copy(w2_hbm, w2_v, load_sem.at[3]),
    ]
    for load in loads:
        load.start()

    barrier = pltpu.get_barrier_semaphore()

    def greet(node, feat):
        pl.semaphore_signal(barrier, inc=1, device_id=(node, feat), device_id_type=MESH)

    for d in range(1, nf):
        greet(n, lax.rem(f + d, nf))
    for d in range(1, nn):
        greet(lax.rem(n + d, nn), f)

    @pl.when(f == 0)
    def _():
        for g in range(nf):
            greet(n_prev, jnp.int32(g))

    @pl.when(f == nf - 1)
    def _():
        for g in range(nf):
            greet(n_next, jnp.int32(g))

    pl.semaphore_wait(barrier, nf + nn)

    partner = f + 1 - 2 * z
    half = nf * fd // 2
    row_own = (f // 2) * fd + z * half
    row_other = (f // 2) * fd + (1 - z) * half

    def columns(j):
        return pl.ds(pl.multiple_of(j * rows, rows), rows)

    far_first = sorted(range(nf), key=lambda t: (abs(t - nf // 2), t))
    for t in far_first:
        j = lax.rem(partner + t, nf)
        remote(feats.at[:, columns(j)], zb.at[:, columns(j)], zsend.at[0], zrecv.at[t], n, partner).start()

    def spread(t, source, row, h):
        j = lax.rem(f + t, nf)
        s = source.at[:, columns(j)]

        def to(part):
            return ft.at[pl.ds(pl.multiple_of(row, fd), fd), pl.ds(part * rows, rows)]

        def keep(part):
            pltpu.make_async_copy(s, to(part), frecv.at[h]).start()

        if t % 2 == 0:
            if t == 0:
                keep(1)
            else:
                remote(s, to(1), fsend.at[h], frecv.at[h], n, j).start()
            return
        dn = jnp.where(j == nf - 1, n_next, n)
        df = lax.rem(j + 1, nf)
        if t == nf - 1:
            @pl.when(f == 0)
            def _():
                remote(s, to(0), fedge.at[h], frecv.at[h], dn, df).start()

            @pl.when(f != 0)
            def _():
                keep(0)
        else:
            remote(s, to(0), fsend.at[h], frecv.at[h], dn, df).start()
        dn = jnp.where(j == 0, n_prev, n)
        df = lax.rem(j + nf - 1, nf)
        if t == 1:
            @pl.when(f == nf - 1)
            def _():
                remote(s, to(2), fedge.at[h], frecv.at[h], dn, df).start()

            @pl.when(f != nf - 1)
            def _():
                keep(2)
        else:
            remote(s, to(2), fsend.at[h], frecv.at[h], dn, df).start()

    for t in far_first:
        spread(t, feats, row_own, 0)

    def pass_on(t):
        drain(zb.at[:, pl.ds(0, rows)], zrecv.at[t])
        spread(t, zb, row_other, 1)

    loads[1].wait()

    def cot_step(i, acc):
        base = pl.multiple_of(i * TILE, TILE)
        c = cot_v[pl.ds(base, TILE), :]
        cot_t[:, pl.ds(base, TILE)] = c.T
        return acc + c.astype(F32).reshape(TILE // 8, 8, hid).sum(0)

    bias_part = lax.fori_loop(0, nb // 2, cot_step, jnp.zeros((8, hid), F32))
    pass_on(far_first[0])
    bias_part = lax.fori_loop(nb // 2, nb, cot_step, bias_part)
    for t in far_first[1:-2]:
        pass_on(t)

    first = (n * nf + f - 1) * nb
    total = nn * nf * nb

    def pick(table, b, k):
        s = src[b, k] - first
        s = jnp.where(s >= total, s - total, s)
        s = jnp.where(s < 0, s + total, s)
        return table[jnp.minimum(s, 3 * nb - 1)]

    def pair(b, k):
        return jnp.concatenate([a_v[b, k], a_v[b, k + 1]], axis=1)

    bound_next = jnp.logical_and(f == nf - 1, lax.rem(n, 2) == 1)
    bound_prev = jnp.logical_and(f == 0, lax.rem(n, 2) == 0)
    out_base = z * (2 * nb)
    in_base = (2 - 2 * z) * nb

    def at_cols(row, base, c):
        return pt.at[pl.ds(pl.multiple_of(row, half), half),
                     pl.ds(pl.multiple_of((base + c * ch) * TILE, cr), cr)]

    def arrange(table, row, h):
        drain(ft.at[pl.ds(0, half)], frecv.at[h])

        def step(i, carry):
            table[i] = ft[pl.ds(pl.multiple_of(row, half), half), pl.ds(pl.multiple_of(i * TILE, TILE), TILE)]
            return carry

        lax.fori_loop(0, 3 * nb, step, 0, unroll=4)

    def one_chunk(table, row, h, c):
        for i in range(ch):
            b = c * ch + i
            acc = None
            for k in range(0, neigh, 2):
                p = dot_nt(jnp.concatenate([pick(table, b, k), pick(table, b, k + 1)], axis=1), pair(b, k))
                acc = p if acc is None else acc + p
            pt[pl.ds(pl.multiple_of(row, half), half),
               pl.ds(pl.multiple_of((nb + b) * TILE, TILE), TILE)] = acc.astype(BF)
        m = h * nch + c
        own = at_cols(row, nb, c)
        remote(own, at_cols(row, out_base, c), psend.at[m], pdir.at[m], n, partner).start()

        @pl.when(bound_next)
        def _():
            remote(own, at_cols(row, 0, c), pbound.at[m], pfwd.at[m], n_next, jnp.int32(0)).start()

        @pl.when(bound_prev)
        def _():
            remote(own, at_cols(row, 2 * nb, c), pbound.at[m], pfwd.at[m], n_prev, jnp.int32(nf - 1)).start()

    skip = jnp.logical_or(jnp.logical_and(f == nf - 2, lax.rem(n, 2) == 1),
                          jnp.logical_and(f == 1, lax.rem(n, 2) == 0))
    fwd_f = lax.rem(f + jnp.where(z == 0, 2, nf - 2), nf)
    fwd_n = jnp.where(f == nf - 2, n_next, jnp.where(f == 1, n_prev, n))

    def forward(h, c):
        m = h * nch + c
        row = (1 - z) * half if h == 0 else z * half
        came = at_cols(row, in_base, c)
        drain(came, pdir.at[m])

        @pl.when(jnp.logical_not(skip))
        def _():
            remote(came, at_cols(row, out_base, c), pfsend.at[m], pfwd.at[m], fwd_n, fwd_f).start()

    arrange(fa, z * half, 0)
    loads[2].wait()
    one_chunk(fa, z * half, 0, 0)
    pass_on(far_first[-2])
    if nch > 1:
        one_chunk(fa, z * half, 0, 1)
    pass_on(far_first[-1])
    if nch > 2:
        lax.fori_loop(2, nch, lambda c, u: (one_chunk(fa, z * half, 0, c), u)[1], 0)
    arrange(fb, (1 - z) * half, 1)

    for c in range(nch):
        forward(0, c)

    def second(c, carry):
        one_chunk(fb, (1 - z) * half, 1, c)
        return carry

    lax.fori_loop(0, nch, second, 0)

    loads[0].wait()
    order = [g * fd for g in range(0, nf, 2)] + [g * fd for g in range(1, nf, 2)]
    w_cat = jnp.concatenate(
        [w1_v[g:g + fd, :hid] for g in order] + [w1_v[g:g + fd, hid:] for g in order], axis=0)
    bias_one = b1[...]

    def hidden(base, count):
        def step(i, carry):
            at = pl.ds(base + i * 2, 2)
            cols = pl.ds(pl.multiple_of((base + i * 2) * TILE, 2 * TILE), 2 * TILE)
            v = dot(jnp.concatenate([ft[:, cols], pt[:, cols]], axis=0).T, w_cat) + bias_one
            hn[at] = jnp.maximum(v, 0.0).astype(BF).reshape(2, TILE, hid)
            return carry

        lax.fori_loop(0, count // 2, step, 0)

    def scatter_nodes(g, r, grad, k):
        for i in range(nn):
            g[i] = grad[i * rp:(i + 1) * rp, :].astype(BF)
        for d in range(1, nn):
            dn = lax.rem(n + d, nn)
            remote(g.at[dn], r.at[n], ars.at[k], arr.at[k], dn, f).start()
        r[n] = g[n]

    def share_feat(g, r, q, k, extra):
        drain(r.at[pl.ds(0, nn - 1)], arr.at[k])
        tot = r[0].astype(F32)
        for i in range(1, nn):
            tot = tot + r[i].astype(F32)
        q[f, 0:rp, :] = tot
        if extra is not None:
            q[f, rp:, :] = extra
        for d in range(1, nf):
            remote(q.at[f], q.at[f], ars.at[k + 1], arr.at[k + 1], n, lax.rem(f + d, nf)).start()

    def gather_nodes(q, half, k):
        drain(q.at[pl.ds(0, nf - 1)], arr.at[k + 1])
        tot = q[0]
        for i in range(1, nf):
            tot = tot + q[i]
        at = pl.ds(pl.multiple_of(half * hid + n * rp, rp), rp)
        gfin[at, :] = tot[0:rp, :].astype(BF)
        for d in range(1, nn):
            remote(gfin.at[at], gfin.at[at], ars.at[k + 2], arr.at[k + 2], lax.rem(n + d, nn), f).start()
        if half == 0:
            bslot[n] = tot[rp:, :]
            for d in range(1, nn):
                remote(bslot.at[n], bslot.at[n], ars.at[6], arr.at[6], lax.rem(n + d, nn), f).start()

    def finish(half, k):
        some = gfin.at[pl.ds(half * hid, (nn - 1) * rp)]
        drain(some, arr.at[k + 2])
        at = pl.ds(half * hid, hid)
        return pltpu.make_async_copy(gfin.at[at], gw_hbm.at[at], load_sem.at[4 + half])

    def halo(c):
        for h in range(2):
            drain(at_cols(0, out_base, c), pfwd.at[h * nch + c])
        hidden(out_base + c * ch, ch)

    hidden(nb, nb)
    for c in range(min(2, nch)):
        forward(1, c)
    scatter_nodes(gt, rt, dot(cot_t[...], hn[nb:2 * nb].reshape(rows, hid)).T, 0)
    for c in range(2, nch):
        forward(1, c)
    hidden(in_base, nb)
    for c in range(nch - 1):
        halo(c)
    share_feat(gt, rt, qt, 0, bias_part)
    halo(nch - 1)

    def two_chunk(c, carry):
        for i in range(ch):
            b = c * ch + i
            at = pl.ds(pl.multiple_of(b * TILE, TILE), TILE)
            acc = None
            for k in range(0, neigh, 2):
                p = dot(pair(b, k), jnp.concatenate([pick(hn, b, k), pick(hn, b, k + 1)], axis=0))
                acc = p if acc is None else acc + p
            mn[at, :] = acc.astype(BF)
        return carry

    lax.fori_loop(0, nch, two_chunk, 0)
    scatter_nodes(gb, rb, dot(cot_t[...], mn[...]).T, 3)

    loads[3].wait()
    bias_two = b2[...]

    def out_chunk(c, carry):
        at = pl.ds(pl.multiple_of(c * cr, cr), cr)
        own = hn[pl.ds(nb + c * ch, ch)].reshape(cr, hid)
        both = jnp.concatenate([own, mn[at, :]], axis=1)
        out_v[at, :] = (dot(both, w2_v[...]) + bias_two).astype(BF)
        pltpu.make_async_copy(out_v.at[at], out_hbm.at[at], out_sem.at[c]).start()
        return carry

    lax.fori_loop(0, nch, out_chunk, 0)
    gather_nodes(qt, 0, 0)

    share_feat(gb, rb, qb, 3, None)

    drain(zb, zsend.at[0])
    for h in range(2):
        drain(ft.at[pl.ds(0, (nf + 1) * fd // 3), :], fsend.at[h])

        @pl.when(jnp.logical_or(f == 0, f == nf - 1))
        def _():
            drain(ft.at[pl.ds(0, fd), pl.ds(0, rows)], fedge.at[h])

    for m in range(2 * nch):
        some = at_cols(0, 0, 0)
        drain(some, psend.at[m])

        @pl.when(jnp.logical_or(bound_next, bound_prev))
        def _():
            drain(some, pbound.at[m])

        @pl.when(jnp.logical_not(skip))
        def _():
            drain(some, pfsend.at[m])

    gather_nodes(qb, 1, 3)
    top = finish(0, 0)
    top.start()
    drain(bslot.at[pl.ds(0, nn - 1)], arr.at[6])
    bias = pltpu.make_async_copy(bslot, gb_hbm, load_sem.at[6])
    bias.start()
    for k, (g, q) in ((0, (gt, qt)), (3, (gb, qb))):
        drain(g.at[pl.ds(0, nn - 1)], ars.at[k])
        drain(q.at[pl.ds(0, nf - 1)], ars.at[k + 1])
        drain(gfin.at[pl.ds(0, (nn - 1) * rp)], ars.at[k + 2])
    drain(bslot.at[pl.ds(0, nn - 1)], ars.at[6])
    for c in range(nch):
        drain(out_v.at[pl.ds(c * cr, cr)], out_sem.at[c])
    bottom = finish(1, 3)
    bottom.start()
    top.wait()
    bias.wait()
    bottom.wait()


def per_device(nn, nf, feats, tile_src, tile_weight, w_one, b_one, w_two, b_two, cotangent):
    fd = feats.shape[0]
    nb, neigh = tile_src.shape
    rows = nb * TILE
    hid = b_one.shape[0]
    features = w_one.shape[0]
    rp = hid // nn
    ch = min(4, nb)
    nch = nb // ch
    anyspace = pl.BlockSpec(memory_space=pl.ANY)
    vm = pl.BlockSpec(memory_space=pltpu.VMEM)
    sm = pl.BlockSpec(memory_space=pltpu.SMEM)
    dma = pltpu.SemaphoreType.DMA
    out, gw, gb = pl.pallas_call(
        functools.partial(kernel, nn, nf, nb, neigh, ch),
        out_shape=(
            jax.ShapeDtypeStruct((rows, hid), BF),
            jax.ShapeDtypeStruct((2 * hid, hid), BF),
            jax.ShapeDtypeStruct((nn, 8, hid), F32),
        ),
        in_specs=[anyspace, sm, anyspace, anyspace, vm, anyspace, vm, anyspace],
        out_specs=(anyspace,) * 3,
        scratch_shapes=[
            pltpu.VMEM((features, 3 * rows), BF),
            pltpu.VMEM((fd, nf * rows), BF),
            pltpu.VMEM((3 * nb, features // 2, TILE), BF),
            pltpu.VMEM((3 * nb, features // 2, TILE), BF),
            pltpu.VMEM(tile_weight.shape, BF),
            pltpu.VMEM((features, 3 * rows), BF),
            pltpu.VMEM((3 * nb, TILE, hid), BF),
            pltpu.VMEM((rows, hid), BF),
            pltpu.VMEM((rows, hid), BF),
            pltpu.VMEM((hid, rows), BF),
            pltpu.VMEM(w_one.shape, BF),
            pltpu.VMEM(w_two.shape, BF),
            pltpu.VMEM((rows, hid), BF),
            pltpu.VMEM((nn, rp, hid), BF),
            pltpu.VMEM((nn, rp, hid), BF),
            pltpu.VMEM((nf, rp + 8, hid), F32),
            pltpu.VMEM((nn, rp, hid), BF),
            pltpu.VMEM((nn, rp, hid), BF),
            pltpu.VMEM((nf, rp, hid), F32),
            pltpu.VMEM((2 * hid, hid), BF),
            pltpu.VMEM((nn, 8, hid), F32),
            dma((7,)), dma((1,)), dma((nf,)), dma((2,)), dma((2,)), dma((2,)),
            dma((2 * nch,)), dma((2 * nch,)), dma((2 * nch,)), dma((2 * nch,)), dma((2 * nch,)),
            dma((7,)), dma((7,)), dma((nch,)),
        ],
        compiler_params=pltpu.CompilerParams(
            collective_id=0, has_side_effects=True, vmem_limit_bytes=56 * 2**20),
        name="sage",
    )(feats, tile_src, tile_weight, w_one, b_one.reshape(1, hid), w_two, b_two.reshape(1, hid), cotangent)
    out, gw, gb = pl.pallas_call(
        hand_over,
        out_shape=(
            jax.ShapeDtypeStruct((rows, hid), BF),
            jax.ShapeDtypeStruct((2 * hid, hid), F32),
            jax.ShapeDtypeStruct((1, hid), F32),
        ),
        in_specs=[vm] * 3,
        out_specs=(vm,) * 3,
        name="hand_over",
    )(out, gw, gb)
    return out, gw, gb.reshape(hid)


def solution(mesh):
    nn, nf = mesh.shape["nodes"], mesh.shape["feat"]
    return jax.shard_map(
        functools.partial(per_device, nn, nf),
        mesh=mesh,
        in_specs=(
            P("feat", "nodes"),
            P(("nodes", "feat"), None),
            P(("nodes", "feat"), None, None, None),
            P(),
            P(),
            P(),
            P(),
            P(("nodes", "feat"), None),
        ),
        out_specs=(P(("nodes", "feat"), None), P(), P()),
        check_vma=False,
    )
```

```python
import functools

import jax
import jax.numpy as jnp
from jax import lax
from jax.experimental import pallas as pl
from jax.experimental.pallas import tpu as pltpu
from jax.sharding import PartitionSpec as P

BF = jnp.bfloat16
F32 = jnp.float32
TILE = 128
MESH = pl.DeviceIdType.MESH


def remote(src, dst, send_sem, recv_sem, node, feat):
    return pltpu.make_async_remote_copy(
        src_ref=src, dst_ref=dst, send_sem=send_sem, recv_sem=recv_sem,
        device_id=(node, feat), device_id_type=MESH)


def drain(ref, sem):
    pltpu.make_async_copy(ref, ref, sem).wait()


def dot(a, b):
    return lax.dot_general(a, b, (((1,), (0,)), ((), ())), preferred_element_type=F32)


def dot_nt(a, b):
    return lax.dot_general(a, b, (((1,), (1,)), ((), ())), preferred_element_type=F32)


def hand_over(out, gw, gb, out_copy, gw_wide, gb_sum):
    out_copy[...] = out[...]
    gw_wide[...] = gw[...].astype(F32)
    tot = gb[0]
    for i in range(1, gb.shape[0]):
        tot = tot + gb[i]
    gb_sum[...] = jnp.sum(tot, axis=0, keepdims=True)


def kernel(nn, nf, nb, neigh, chunk_blocks,
           feats, src, a_hbm, w1_hbm, b1, w2_hbm, b2, cot_hbm,
           out_hbm, gw_hbm, gb_hbm,
           ft, zb, fa, fb, a_v, pt, hn, mn, cot_v, cot_t, w1_v, w2_v, out_v,
           gt, rt, qt, gb, rb, qb, gfin, bslot, g_acc,
           load_sem, zsend, zrecv, fsend, fedge, frecv, psend, pbound, pfsend, pdir, pfwd,
           ars, arr, out_sem):
    fd = feats.shape[0]
    rows = nb * TILE
    hid = b1.shape[1]
    rp = hid // nn
    ch = chunk_blocks
    nch = nb // ch
    cr = ch * TILE
    plan = ([(c * ch, ch) for c in range(nch)],
            [(c * ch, ch) for c in range(nch - 1)] + [(nb - ch, ch // 2), (nb - ch // 2, ch // 2)])
    last = nch
    n = lax.axis_index("nodes")
    f = lax.axis_index("feat")
    z = lax.rem(f, 2)
    n_next = lax.rem(n + 1, nn)
    n_prev = lax.rem(n + nn - 1, nn)

    loads = [
        pltpu.make_async_copy(w1_hbm, w1_v, load_sem.at[0]),
        pltpu.make_async_copy(cot_hbm, cot_v, load_sem.at[1]),
        pltpu.make_async_copy(a_hbm, a_v, load_sem.at[2]),
        pltpu.make_async_copy(w2_hbm, w2_v, load_sem.at[3]),
    ]
    for load in loads:
        load.start()

    barrier = pltpu.get_barrier_semaphore()

    def greet(node, feat):
        pl.semaphore_signal(barrier, inc=1, device_id=(node, feat), device_id_type=MESH)

    for d in range(1, nf):
        greet(n, lax.rem(f + d, nf))
    for d in range(1, nn):
        greet(lax.rem(n + d, nn), f)

    @pl.when(f == 0)
    def _():
        for g in range(nf):
            greet(n_prev, jnp.int32(g))

    @pl.when(f == nf - 1)
    def _():
        for g in range(nf):
            greet(n_next, jnp.int32(g))

    pl.semaphore_wait(barrier, nf + nn)

    partner = f + 1 - 2 * z
    half = nf * fd // 2
    row_own = (f // 2) * fd + z * half
    row_other = (f // 2) * fd + (1 - z) * half

    def columns(j):
        return pl.ds(pl.multiple_of(j * rows, rows), rows)

    far_first = sorted(range(nf), key=lambda t: (abs(t - nf // 2), t))
    for t in far_first:
        j = lax.rem(partner + t, nf)
        remote(feats.at[:, columns(j)], zb.at[:, columns(j)], zsend.at[0], zrecv.at[t], n, partner).start()

    def spread(t, source, row, h):
        j = lax.rem(f + t, nf)
        s = source.at[:, columns(j)]

        def to(part):
            return ft.at[pl.ds(pl.multiple_of(row, fd), fd), pl.ds(part * rows, rows)]

        def keep(part):
            pltpu.make_async_copy(s, to(part), frecv.at[h]).start()

        if t % 2 == 0:
            if t == 0:
                keep(1)
            else:
                remote(s, to(1), fsend.at[h], frecv.at[h], n, j).start()
            return
        dn = jnp.where(j == nf - 1, n_next, n)
        df = lax.rem(j + 1, nf)
        if t == nf - 1:
            @pl.when(f == 0)
            def _():
                remote(s, to(0), fedge.at[h], frecv.at[h], dn, df).start()

            @pl.when(f != 0)
            def _():
                keep(0)
        else:
            remote(s, to(0), fsend.at[h], frecv.at[h], dn, df).start()
        dn = jnp.where(j == 0, n_prev, n)
        df = lax.rem(j + nf - 1, nf)
        if t == 1:
            @pl.when(f == nf - 1)
            def _():
                remote(s, to(2), fedge.at[h], frecv.at[h], dn, df).start()

            @pl.when(f != nf - 1)
            def _():
                keep(2)
        else:
            remote(s, to(2), fsend.at[h], frecv.at[h], dn, df).start()

    for t in far_first:
        spread(t, feats, row_own, 0)

    def pass_on(t):
        drain(zb.at[:, pl.ds(0, rows)], zrecv.at[t])
        spread(t, zb, row_other, 1)

    loads[1].wait()

    def cot_step(i, acc):
        base = pl.multiple_of(i * TILE, TILE)
        c = cot_v[pl.ds(base, TILE), :]
        cot_t[:, pl.ds(base, TILE)] = c.T
        return acc + c.astype(F32).reshape(TILE // 8, 8, hid).sum(0)

    bias_part = lax.fori_loop(0, nb // 2, cot_step, jnp.zeros((8, hid), F32))
    pass_on(far_first[0])
    bias_part = lax.fori_loop(nb // 2, nb, cot_step, bias_part)
    for t in far_first[1:-2]:
        pass_on(t)

    first = (n * nf + f - 1) * nb
    total = nn * nf * nb

    def pick(table, b, k):
        s = src[b, k] - first
        s = jnp.where(s >= total, s - total, s)
        s = jnp.where(s < 0, s + total, s)
        return table[jnp.minimum(s, 3 * nb - 1)]

    def pair(b, k):
        return jnp.concatenate([a_v[b, k], a_v[b, k + 1]], axis=1)

    bound_next = jnp.logical_and(f == nf - 1, lax.rem(n, 2) == 1)
    bound_prev = jnp.logical_and(f == 0, lax.rem(n, 2) == 0)
    out_base = z * (2 * nb)
    in_base = (2 - 2 * z) * nb

    def at_cols(row, block, count):
        return pt.at[pl.ds(pl.multiple_of(row, half), half),
                     pl.ds(pl.multiple_of(block * TILE, count * TILE), count * TILE)]

    def arrange(table, row, h):
        drain(ft.at[pl.ds(0, half)], frecv.at[h])

        def step(i, carry):
            table[i] = ft[pl.ds(pl.multiple_of(row, half), half), pl.ds(pl.multiple_of(i * TILE, TILE), TILE)]
            return carry

        lax.fori_loop(0, 3 * nb, step, 0, unroll=4)

    direct_f = lax.rem(f + jnp.where(z == 0, nf - 1, 1), nf)
    direct_n = jnp.where(f == 0, n_prev, jnp.where(f == nf - 1, n_next, n))
    direct_base = (2 - 2 * z) * nb

    def one_chunk(table, row, h, m, block, count):
        for i in range(count):
            b = block + i
            acc = None
            for k in range(0, neigh, 2):
                p = dot_nt(jnp.concatenate([pick(table, b, k), pick(table, b, k + 1)], axis=1), pair(b, k))
                acc = p if acc is None else acc + p
            pt[pl.ds(pl.multiple_of(row, half), half),
               pl.ds(pl.multiple_of((nb + b) * TILE, TILE), TILE)] = acc.astype(BF)
        own = at_cols(row, nb + block, count)
        remote(own, at_cols(row, out_base + block, count), psend.at[m], pdir.at[m], n, partner).start()

        def direct():
            remote(own, at_cols(row, direct_base + block, count), pbound.at[m], pfwd.at[m],
                   direct_n, direct_f).start()

        if h == 1 and count < ch:
            if block == nb - count:
                direct()
                return

        pl.when(jnp.logical_or(bound_next, bound_prev))(direct)

    skip = jnp.logical_or(jnp.logical_and(f == nf - 2, lax.rem(n, 2) == 1),
                          jnp.logical_and(f == 1, lax.rem(n, 2) == 0))
    fwd_f = lax.rem(f + jnp.where(z == 0, 2, nf - 2), nf)
    fwd_n = jnp.where(f == nf - 2, n_next, jnp.where(f == 1, n_prev, n))

    def forward(h, c):
        m = h * nch + c
        block, count = plan[h][c]
        row = (1 - z) * half if h == 0 else z * half
        came = at_cols(row, in_base + block, count)
        drain(came, pdir.at[m])
        if h == 1 and c == last:
            return

        @pl.when(jnp.logical_not(skip))
        def _():
            remote(came, at_cols(row, out_base + block, count), pfsend.at[m], pfwd.at[m], fwd_n, fwd_f).start()

    arrange(fa, z * half, 0)
    loads[2].wait()
    one_chunk(fa, z * half, 0, 0, 0, ch)
    pass_on(far_first[-2])
    if nch > 1:
        one_chunk(fa, z * half, 0, 1, ch, ch)
    pass_on(far_first[-1])
    if nch > 2:
        lax.fori_loop(2, nch, lambda c, u: (one_chunk(fa, z * half, 0, c, c * ch, ch), u)[1], 0)
    arrange(fb, (1 - z) * half, 1)
    for c in range(nch):
        forward(0, c)

    if nch > 1:
        lax.fori_loop(0, nch - 1, lambda c, u: (one_chunk(fb, (1 - z) * half, 1, nch + c, c * ch, ch), u)[1], 0)
    for c in (nch - 1, nch):
        one_chunk(fb, (1 - z) * half, 1, nch + c, *plan[1][c])

    loads[0].wait()
    order = [g * fd for g in range(0, nf, 2)] + [g * fd for g in range(1, nf, 2)]
    w_cat = jnp.concatenate(
        [w1_v[g:g + fd, :hid] for g in order] + [w1_v[g:g + fd, hid:] for g in order], axis=0)
    bias_one = b1[...]

    def hidden(base, count):
        def step(i, carry):
            at = pl.ds(base + i * 2, 2)
            cols = pl.ds(pl.multiple_of((base + i * 2) * TILE, 2 * TILE), 2 * TILE)
            v = dot(jnp.concatenate([ft[:, cols], pt[:, cols]], axis=0).T, w_cat) + bias_one
            hn[at] = jnp.maximum(v, 0.0).astype(BF).reshape(2, TILE, hid)
            return carry

        lax.fori_loop(0, count // 2, step, 0)

    def scatter_nodes(g, r, grad, k):
        for i in range(nn):
            g[i] = grad[i * rp:(i + 1) * rp, :].astype(BF)
        for d in range(1, nn):
            dn = lax.rem(n + d, nn)
            remote(g.at[dn], r.at[n], ars.at[k], arr.at[k], dn, f).start()
        r[n] = g[n]

    def share_feat(g, r, q, k, extra):
        drain(r.at[pl.ds(0, nn - 1)], arr.at[k])
        tot = r[0].astype(F32)
        for i in range(1, nn):
            tot = tot + r[i].astype(F32)
        q[f, 0:rp, :] = tot
        if extra is not None:
            q[f, rp:, :] = extra
        for d in range(1, nf):
            remote(q.at[f], q.at[f], ars.at[k + 1], arr.at[k + 1], n, lax.rem(f + d, nf)).start()

    def gather_nodes(q, half, k):
        drain(q.at[pl.ds(0, nf - 1)], arr.at[k + 1])
        tot = q[0]
        for i in range(1, nf):
            tot = tot + q[i]
        at = pl.ds(pl.multiple_of(half * hid + n * rp, rp), rp)
        gfin[at, :] = tot[0:rp, :].astype(BF)
        for d in range(1, nn):
            remote(gfin.at[at], gfin.at[at], ars.at[k + 2], arr.at[k + 2], lax.rem(n + d, nn), f).start()
        if half == 0:
            bslot[n] = tot[rp:, :]
            for d in range(1, nn):
                remote(bslot.at[n], bslot.at[n], ars.at[6], arr.at[6], lax.rem(n + d, nn), f).start()

    def finish(half, k):
        some = gfin.at[pl.ds(half * hid, (nn - 1) * rp)]
        drain(some, arr.at[k + 2])
        at = pl.ds(half * hid, hid)
        return pltpu.make_async_copy(gfin.at[at], gw_hbm.at[at], load_sem.at[4 + half])

    def halo(c):
        block, count = plan[1][c]
        if c < nch:
            drain(at_cols(0, *plan[0][c]), pfwd.at[c])
        drain(at_cols(0, block, count), pfwd.at[nch + c])
        hidden(out_base + block, count)

    hidden(nb, nb)
    for c in range(min(2, nch)):
        forward(1, c)
    scatter_nodes(gt, rt, dot(cot_t[...], hn[nb:2 * nb].reshape(rows, hid)).T, 0)
    for c in range(2, nch + 1):
        forward(1, c)
    hidden(in_base, nb)
    for c in range(nch - 1):
        halo(c)
    share_feat(gt, rt, qt, 0, bias_part)
    halo(nch - 1)
    halo(nch)

    def two_chunk(c, carry):
        turned = []
        for i in range(ch):
            b = c * ch + i
            at = pl.ds(pl.multiple_of(b * TILE, TILE), TILE)
            acc = None
            for k in range(0, neigh, 2):
                p = dot(pair(b, k), jnp.concatenate([pick(hn, b, k), pick(hn, b, k + 1)], axis=0))
                acc = p if acc is None else acc + p
            mixed = acc.astype(BF)
            mn[at, :] = mixed
            turned.append(mixed.T)
        at = pl.ds(pl.multiple_of(c * cr, cr), cr)
        g_acc[...] += dot(jnp.concatenate(turned, axis=1), cot_v[at, :])
        return carry

    g_acc[...] = jnp.zeros_like(g_acc)
    lax.fori_loop(0, nch, two_chunk, 0)
    scatter_nodes(gb, rb, g_acc[...], 3)

    loads[3].wait()
    bias_two = b2[...]

    def out_chunk(c, carry):
        at = pl.ds(pl.multiple_of(c * cr, cr), cr)
        own = hn[pl.ds(nb + c * ch, ch)].reshape(cr, hid)
        both = jnp.concatenate([own, mn[at, :]], axis=1)
        out_v[at, :] = (dot(both, w2_v[...]) + bias_two).astype(BF)
        pltpu.make_async_copy(out_v.at[at], out_hbm.at[at], out_sem.at[c]).start()
        return carry

    lax.fori_loop(0, nch, out_chunk, 0)
    gather_nodes(qt, 0, 0)

    share_feat(gb, rb, qb, 3, None)

    drain(zb, zsend.at[0])
    for h in range(2):
        drain(ft.at[pl.ds(0, (nf + 1) * fd // 3), :], fsend.at[h])

        @pl.when(jnp.logical_or(f == 0, f == nf - 1))
        def _():
            drain(ft.at[pl.ds(0, fd), pl.ds(0, rows)], fedge.at[h])

    for h in range(2):
        for c in range(nch + h):
            m = h * nch + c
            some = at_cols(0, *plan[h][c])
            drain(some, psend.at[m])
            if h == 1 and c == last:
                drain(some, pbound.at[m])
                continue

            @pl.when(jnp.logical_or(bound_next, bound_prev))
            def _():
                drain(some, pbound.at[m])

            @pl.when(jnp.logical_not(skip))
            def _():
                drain(some, pfsend.at[m])

    gather_nodes(qb, 1, 3)
    top = finish(0, 0)
    top.start()
    drain(bslot.at[pl.ds(0, nn - 1)], arr.at[6])
    bias = pltpu.make_async_copy(bslot, gb_hbm, load_sem.at[6])
    bias.start()
    for k, (g, q) in ((0, (gt, qt)), (3, (gb, qb))):
        drain(g.at[pl.ds(0, nn - 1)], ars.at[k])
        drain(q.at[pl.ds(0, nf - 1)], ars.at[k + 1])
        drain(gfin.at[pl.ds(0, (nn - 1) * rp)], ars.at[k + 2])
    drain(bslot.at[pl.ds(0, nn - 1)], ars.at[6])
    for c in range(nch):
        drain(out_v.at[pl.ds(c * cr, cr)], out_sem.at[c])
    bottom = finish(1, 3)
    bottom.start()
    top.wait()
    bias.wait()
    bottom.wait()


def per_device(nn, nf, feats, tile_src, tile_weight, w_one, b_one, w_two, b_two, cotangent):
    fd = feats.shape[0]
    nb, neigh = tile_src.shape
    rows = nb * TILE
    hid = b_one.shape[0]
    features = w_one.shape[0]
    rp = hid // nn
    ch = min(4, nb)
    nch = nb // ch
    anyspace = pl.BlockSpec(memory_space=pl.ANY)
    vm = pl.BlockSpec(memory_space=pltpu.VMEM)
    sm = pl.BlockSpec(memory_space=pltpu.SMEM)
    dma = pltpu.SemaphoreType.DMA
    out, gw, gb = pl.pallas_call(
        functools.partial(kernel, nn, nf, nb, neigh, ch),
        out_shape=(
            jax.ShapeDtypeStruct((rows, hid), BF),
            jax.ShapeDtypeStruct((2 * hid, hid), BF),
            jax.ShapeDtypeStruct((nn, 8, hid), F32),
        ),
        in_specs=[anyspace, sm, anyspace, anyspace, vm, anyspace, vm, anyspace],
        out_specs=(anyspace,) * 3,
        scratch_shapes=[
            pltpu.VMEM((features, 3 * rows), BF),
            pltpu.VMEM((fd, nf * rows), BF),
            pltpu.VMEM((3 * nb, features // 2, TILE), BF),
            pltpu.VMEM((3 * nb, features // 2, TILE), BF),
            pltpu.VMEM(tile_weight.shape, BF),
            pltpu.VMEM((features, 3 * rows), BF),
            pltpu.VMEM((3 * nb, TILE, hid), BF),
            pltpu.VMEM((rows, hid), BF),
            pltpu.VMEM((rows, hid), BF),
            pltpu.VMEM((hid, rows), BF),
            pltpu.VMEM(w_one.shape, BF),
            pltpu.VMEM(w_two.shape, BF),
            pltpu.VMEM((rows, hid), BF),
            pltpu.VMEM((nn, rp, hid), BF),
            pltpu.VMEM((nn, rp, hid), BF),
            pltpu.VMEM((nf, rp + 8, hid), F32),
            pltpu.VMEM((nn, rp, hid), BF),
            pltpu.VMEM((nn, rp, hid), BF),
            pltpu.VMEM((nf, rp, hid), F32),
            pltpu.VMEM((2 * hid, hid), BF),
            pltpu.VMEM((nn, 8, hid), F32),
            pltpu.VMEM((hid, hid), F32),
            dma((7,)), dma((1,)), dma((nf,)), dma((2,)), dma((2,)), dma((2,)),
            dma((2 * nch + 1,)), dma((2 * nch + 1,)), dma((2 * nch + 1,)), dma((2 * nch + 1,)), dma((2 * nch + 1,)),
            dma((7,)), dma((7,)), dma((nch,)),
        ],
        compiler_params=pltpu.CompilerParams(
            collective_id=0, has_side_effects=True, vmem_limit_bytes=56 * 2**20),
        name="sage",
    )(feats, tile_src, tile_weight, w_one, b_one.reshape(1, hid), w_two, b_two.reshape(1, hid), cotangent)
    out, gw, gb = pl.pallas_call(
        hand_over,
        out_shape=(
            jax.ShapeDtypeStruct((rows, hid), BF),
            jax.ShapeDtypeStruct((2 * hid, hid), F32),
            jax.ShapeDtypeStruct((1, hid), F32),
        ),
        in_specs=[vm] * 3,
        out_specs=(vm,) * 3,
        name="hand_over",
    )(out, gw, gb)
    return out, gw, gb.reshape(hid)


def solution(mesh):
    nn, nf = mesh.shape["nodes"], mesh.shape["feat"]
    return jax.shard_map(
        functools.partial(per_device, nn, nf),
        mesh=mesh,
        in_specs=(
            P("feat", "nodes"),
            P(("nodes", "feat"), None),
            P(("nodes", "feat"), None, None, None),
            P(),
            P(),
            P(),
            P(),
            P(("nodes", "feat"), None),
        ),
        out_specs=(P(("nodes", "feat"), None), P(), P()),
        check_vma=False,
    )
```

```python
import functools

import jax
import jax.numpy as jnp
from jax import lax
from jax.experimental import pallas as pl
from jax.experimental.pallas import tpu as pltpu
from jax.sharding import PartitionSpec as P

BF = jnp.bfloat16
F32 = jnp.float32
TILE = 128
MESH = pl.DeviceIdType.MESH


def remote(src, dst, send_sem, recv_sem, node, feat):
    return pltpu.make_async_remote_copy(
        src_ref=src, dst_ref=dst, send_sem=send_sem, recv_sem=recv_sem,
        device_id=(node, feat), device_id_type=MESH)


def drain(ref, sem):
    pltpu.make_async_copy(ref, ref, sem).wait()


def dot(a, b):
    return lax.dot_general(a, b, (((1,), (0,)), ((), ())), preferred_element_type=F32)


def dot_nt(a, b):
    return lax.dot_general(a, b, (((1,), (1,)), ((), ())), preferred_element_type=F32)


def hand_over(out, gw, gb, out_copy, gw_wide, gb_sum):
    out_copy[...] = out[...]
    gw_wide[...] = gw[...].astype(F32)
    tot = gb[0]
    for i in range(1, gb.shape[0]):
        tot = tot + gb[i]
    gb_sum[...] = jnp.sum(tot, axis=0, keepdims=True)


def kernel(nn, nf, nb, neigh, chunk_blocks,
           feats, src, a_hbm, w1_hbm, b1, w2_hbm, b2, cot_hbm,
           out_hbm, gw_hbm, gb_hbm,
           ft, zb, fa, fb, a_v, pt, hn, mn, cot_v, cot_t, w1_v, w2_v, out_v,
           gt, rt, qt, gb, rb, qb, gfin, bslot, g_acc, loc,
           load_sem, zsend, zrecv, fsend, fedge, fextra, frecv, psend, pbound, pfsend, pdir, pfwd,
           ars, arr, out_sem):
    fd = feats.shape[0]
    rows = nb * TILE
    hid = b1.shape[1]
    rp = hid // nn
    ch = chunk_blocks
    nch = nb // ch
    cr = ch * TILE
    plan = ([(c * ch, ch) for c in range(nch)],
            [(c * ch, ch) for c in range(nch - 1)] + [(nb - ch, ch // 2), (nb - ch // 2, ch // 2)])
    straight_set = ((1, nch),)
    n = lax.axis_index("nodes")
    f = lax.axis_index("feat")
    z = lax.rem(f, 2)
    n_next = lax.rem(n + 1, nn)
    n_prev = lax.rem(n + nn - 1, nn)

    loads = [
        pltpu.make_async_copy(w1_hbm, w1_v, load_sem.at[0]),
        pltpu.make_async_copy(cot_hbm, cot_v, load_sem.at[1]),
        pltpu.make_async_copy(a_hbm, a_v, load_sem.at[2]),
        pltpu.make_async_copy(w2_hbm, w2_v, load_sem.at[3]),
    ]
    for load in loads:
        load.start()

    barrier = pltpu.get_barrier_semaphore()

    def greet(node, feat):
        pl.semaphore_signal(barrier, inc=1, device_id=(node, feat), device_id_type=MESH)

    for d in range(1, nf):
        greet(n, lax.rem(f + d, nf))
    for d in range(1, nn):
        greet(lax.rem(n + d, nn), f)

    @pl.when(f == 0)
    def _():
        for g in range(nf):
            greet(n_prev, jnp.int32(g))

    @pl.when(f == nf - 1)
    def _():
        for g in range(nf):
            greet(n_next, jnp.int32(g))

    pl.semaphore_wait(barrier, nf + nn)

    partner = f + 1 - 2 * z
    half = nf * fd // 2
    row_own = (f // 2) * fd + z * half
    row_other = (f // 2) * fd + (1 - z) * half

    def columns(j):
        return pl.ds(pl.multiple_of(j * rows, rows), rows)

    far_first = sorted(range(nf), key=lambda t: (abs(t - nf // 2), t))
    for t in far_first:
        j = lax.rem(partner + t, nf)
        remote(feats.at[:, columns(j)], zb.at[:, columns(j)], zsend.at[0], zrecv.at[t], n, partner).start()

    cross = lax.rem(n + f, 2) == 1

    def spread(t, source, row, h):
        j = lax.rem(f + t, nf)
        s = source.at[:, columns(j)]

        def to(part):
            return ft.at[pl.ds(pl.multiple_of(row, fd), fd), pl.ds(part * rows, rows)]

        def keep(part):
            pltpu.make_async_copy(s, to(part), frecv.at[h]).start()

        def send(part, node, feat):
            remote(s, to(part), fsend.at[h], frecv.at[h], node, feat).start()

        def over(part, node, feat, sem, recv):
            remote(s, to(part), sem, frecv.at[recv], node, jnp.int32(feat)).start()

        if t % 2 == 0:
            if t == 0:
                keep(1)
            else:
                send(1, n, j)
            if h == 0:
                pl.when(jnp.logical_and(j == nf - 1, lax.rem(n, 2) == 1))(
                    lambda: over(0, n_next, 0, fextra.at[0], 1))
                pl.when(jnp.logical_and(j == 0, lax.rem(n, 2) == 0))(
                    lambda: over(2, n_prev, nf - 1, fextra.at[0], 1))
            return
        ours = True if h == 0 else jnp.logical_not(cross)
        for part, at_edge, step, node, feat, own in ((0, j == nf - 1, 1, n_next, 0, nf - 1),
                                                     (2, j == 0, nf - 1, n_prev, nf - 1, 1)):
            pl.when(jnp.logical_and(at_edge, ours))(
                functools.partial(over, part, node, feat, fedge.at[h], h))
            inside = functools.partial(keep, part) if t == own else functools.partial(
                send, part, n, lax.rem(j + step, nf))
            pl.when(jnp.logical_not(at_edge))(inside)

    for t in far_first:
        spread(t, feats, row_own, 0)

    def pass_on(t):
        drain(zb.at[:, pl.ds(0, rows)], zrecv.at[t])
        spread(t, zb, row_other, 1)

    loads[1].wait()

    def cot_step(i, acc):
        base = pl.multiple_of(i * TILE, TILE)
        c = cot_v[pl.ds(base, TILE), :]
        cot_t[:, pl.ds(base, TILE)] = c.T
        return acc + c.astype(F32).reshape(TILE // 8, 8, hid).sum(0)

    bias_part = lax.fori_loop(0, nb // 2, cot_step, jnp.zeros((8, hid), F32))
    pass_on(far_first[0])
    bias_part = lax.fori_loop(nb // 2, nb, cot_step, bias_part)
    for t in far_first[1:-2]:
        pass_on(t)

    first = (n * nf + f - 1) * nb
    total = nn * nf * nb

    def locate(b, carry):
        for k in range(neigh):
            s = src[b, k] - first
            s = jnp.where(s >= total, s - total, s)
            s = jnp.where(s < 0, s + total, s)
            loc[b, k] = jnp.minimum(s, 3 * nb - 1)
        return carry

    def pick(table, b, k):
        return table[loc[b, k]]

    def pair(b, k):
        return jnp.concatenate([a_v[b, k], a_v[b, k + 1]], axis=1)

    bound_next = jnp.logical_and(f == nf - 1, lax.rem(n, 2) == 1)
    bound_prev = jnp.logical_and(f == 0, lax.rem(n, 2) == 0)
    out_base = z * (2 * nb)
    in_base = (2 - 2 * z) * nb

    def at_cols(row, block, count):
        return pt.at[pl.ds(pl.multiple_of(row, half), half),
                     pl.ds(pl.multiple_of(block * TILE, count * TILE), count * TILE)]

    def arrange(table, row, h):
        drain(ft.at[pl.ds(0, half)], frecv.at[h])

        def step(i, carry):
            table[i] = ft[pl.ds(pl.multiple_of(row, half), half), pl.ds(pl.multiple_of(i * TILE, TILE), TILE)]
            return carry

        lax.fori_loop(0, 3 * nb, step, 0, unroll=4)

    direct_f = lax.rem(f + jnp.where(z == 0, nf - 1, 1), nf)
    direct_n = jnp.where(f == 0, n_prev, jnp.where(f == nf - 1, n_next, n))
    direct_base = (2 - 2 * z) * nb

    def one_chunk(table, row, h, m, block, count, straight=False):
        for i in range(count):
            b = block + i
            acc = None
            for k in range(0, neigh, 2):
                p = dot_nt(jnp.concatenate([pick(table, b, k), pick(table, b, k + 1)], axis=1), pair(b, k))
                acc = p if acc is None else acc + p
            pt[pl.ds(pl.multiple_of(row, half), half),
               pl.ds(pl.multiple_of((nb + b) * TILE, TILE), TILE)] = acc.astype(BF)
        own = at_cols(row, nb + block, count)
        remote(own, at_cols(row, out_base + block, count), psend.at[m], pdir.at[m], n, partner).start()

        def direct():
            remote(own, at_cols(row, direct_base + block, count), pbound.at[m], pfwd.at[m],
                   direct_n, direct_f).start()

        if straight:
            direct()
        else:
            pl.when(jnp.logical_or(bound_next, bound_prev))(direct)

    skip = jnp.logical_or(jnp.logical_and(f == nf - 2, lax.rem(n, 2) == 1),
                          jnp.logical_and(f == 1, lax.rem(n, 2) == 0))
    fwd_f = lax.rem(f + jnp.where(z == 0, 2, nf - 2), nf)
    fwd_n = jnp.where(f == nf - 2, n_next, jnp.where(f == 1, n_prev, n))

    def forward(h, c):
        m = h * nch + c
        block, count = plan[h][c]
        row = (1 - z) * half if h == 0 else z * half
        came = at_cols(row, in_base + block, count)
        drain(came, pdir.at[m])
        if (h, c) in straight_set:
            return

        @pl.when(jnp.logical_not(skip))
        def _():
            remote(came, at_cols(row, out_base + block, count), pfsend.at[m], pfwd.at[m], fwd_n, fwd_f).start()

    lax.fori_loop(0, nb, locate, 0)
    arrange(fa, z * half, 0)
    loads[2].wait()
    one_chunk(fa, z * half, 0, 0, 0, ch, (0, 0) in straight_set)
    pass_on(far_first[-2])
    if nch > 1:
        one_chunk(fa, z * half, 0, 1, ch, ch, (0, 1) in straight_set)
    pass_on(far_first[-1])
    if nch > 2:
        lax.fori_loop(2, nch, lambda c, u: (one_chunk(fa, z * half, 0, c, c * ch, ch, (0, 2) in straight_set), u)[1], 0)
    arrange(fb, (1 - z) * half, 1)
    for c in range(nch):
        forward(0, c)

    if nch > 1:
        lax.fori_loop(0, nch - 1, lambda c, u: (one_chunk(fb, (1 - z) * half, 1, nch + c, c * ch, ch), u)[1], 0)
    for c in (nch - 1, nch):
        one_chunk(fb, (1 - z) * half, 1, nch + c, *plan[1][c], (1, c) in straight_set)

    loads[0].wait()
    order = [g * fd for g in range(0, nf, 2)] + [g * fd for g in range(1, nf, 2)]
    w_cat = jnp.concatenate(
        [w1_v[g:g + fd, :hid] for g in order] + [w1_v[g:g + fd, hid:] for g in order], axis=0)
    bias_one = b1[...]

    def hidden(base, count):
        def step(i, carry):
            at = pl.ds(base + i * 2, 2)
            cols = pl.ds(pl.multiple_of((base + i * 2) * TILE, 2 * TILE), 2 * TILE)
            v = dot(jnp.concatenate([ft[:, cols], pt[:, cols]], axis=0).T, w_cat) + bias_one
            hn[at] = jnp.maximum(v, 0.0).astype(BF).reshape(2, TILE, hid)
            return carry

        lax.fori_loop(0, count // 2, step, 0, unroll=min(4, count // 2))

    def pieces(g, grad):
        for i in range(nn):
            g[i] = grad[i * rp:(i + 1) * rp, :].astype(BF)

    def scatter_nodes(g, r, k):
        for d in range(1, nn):
            dn = lax.rem(n + d, nn)
            remote(g.at[dn], r.at[n], ars.at[k], arr.at[k], dn, f).start()
        r[n] = g[n]

    def share_feat(g, r, q, k, extra):
        drain(r.at[pl.ds(0, nn - 1)], arr.at[k])
        tot = r[0].astype(F32)
        for i in range(1, nn):
            tot = tot + r[i].astype(F32)
        q[f, 0:rp, :] = tot
        if extra is not None:
            q[f, rp:, :] = extra
        for d in range(1, nf):
            remote(q.at[f], q.at[f], ars.at[k + 1], arr.at[k + 1], n, lax.rem(f + d, nf)).start()

    def gather_nodes(q, half, k):
        drain(q.at[pl.ds(0, nf - 1)], arr.at[k + 1])
        tot = q[0]
        for i in range(1, nf):
            tot = tot + q[i]
        at = pl.ds(pl.multiple_of(half * hid + n * rp, rp), rp)
        gfin[at, :] = tot[0:rp, :].astype(BF)
        for d in range(1, nn):
            remote(gfin.at[at], gw_hbm.at[at], ars.at[k + 2], arr.at[k + 2], lax.rem(n + d, nn), f).start()
        pltpu.make_async_copy(gfin.at[at], gw_hbm.at[at], load_sem.at[4 + half]).start()
        if half == 0:
            bslot[n] = tot[rp:, :]
            for d in range(1, nn):
                remote(bslot.at[n], gb_hbm.at[n], ars.at[6], arr.at[6], lax.rem(n + d, nn), f).start()
            pltpu.make_async_copy(bslot.at[n], gb_hbm.at[n], load_sem.at[6]).start()

    def halo(c):
        block, count = plan[1][c]
        if c < nch:
            drain(at_cols(0, *plan[0][c]), pfwd.at[c])
        drain(at_cols(0, block, count), pfwd.at[nch + c])
        hidden(out_base + block, count)

    forward(1, 0)
    hidden(nb, nb)
    forward(1, 1)
    pieces(gt, dot(cot_t[...], hn[nb:2 * nb].reshape(rows, hid)).T)
    for c in range(2, nch):
        forward(1, c)
        if c == 2:
            hidden(in_base, nb // 2)
    scatter_nodes(gt, rt, 0)
    forward(1, nch)
    if nch > 2:
        hidden(in_base + nb // 2, nb // 2)
    else:
        hidden(in_base, nb)
    for c in range(nch + 1):
        halo(c)

    def two_chunk(c, carry):
        turned = []
        for i in range(ch):
            b = c * ch + i
            at = pl.ds(pl.multiple_of(b * TILE, TILE), TILE)
            acc = None
            for k in range(0, neigh, 2):
                p = dot(pair(b, k), jnp.concatenate([pick(hn, b, k), pick(hn, b, k + 1)], axis=0))
                acc = p if acc is None else acc + p
            mixed = acc.astype(BF)
            mn[at, :] = mixed
            turned.append(mixed.T)
        at = pl.ds(pl.multiple_of(c * cr, cr), cr)
        g_acc[...] += dot(jnp.concatenate(turned, axis=1), cot_v[at, :])
        return carry

    g_acc[...] = jnp.zeros_like(g_acc)
    lax.fori_loop(0, nch - 1, two_chunk, 0)
    share_feat(gt, rt, qt, 0, bias_part)
    two_chunk(nch - 1, 0)
    pieces(gb, g_acc[...])
    scatter_nodes(gb, rb, 3)

    loads[3].wait()
    bias_two = b2[...]

    def out_chunk(c, carry):
        at = pl.ds(pl.multiple_of(c * cr, cr), cr)
        own = hn[pl.ds(nb + c * ch, ch)].reshape(cr, hid)
        both = jnp.concatenate([own, mn[at, :]], axis=1)
        out_v[at, :] = (dot(both, w2_v[...]) + bias_two).astype(BF)
        pltpu.make_async_copy(out_v.at[at], out_hbm.at[at], out_sem.at[c]).start()
        return carry

    lax.fori_loop(0, nch, out_chunk, 0)
    gather_nodes(qt, 0, 0)

    share_feat(gb, rb, qb, 3, None)

    drain(zb, zsend.at[0])
    piece = ft.at[pl.ds(0, fd), pl.ds(0, rows)]
    ends = jnp.logical_or(f == 0, f == nf - 1)
    for h in range(2):
        @pl.when(ends)
        def _():
            drain(ft.at[pl.ds(0, (nf + 1) * fd // 3), :], fsend.at[h])

        @pl.when(jnp.logical_not(ends))
        def _():
            drain(zb, fsend.at[h])

    drain(piece, fedge.at[0])

    @pl.when(jnp.logical_not(cross))
    def _():
        drain(piece, fedge.at[1])
        drain(piece, fextra.at[0])

    for h in range(2):
        for c in range(nch + h):
            m = h * nch + c
            some = at_cols(0, *plan[h][c])
            drain(some, psend.at[m])
            if (h, c) in straight_set:
                drain(some, pbound.at[m])
                continue

            @pl.when(jnp.logical_or(bound_next, bound_prev))
            def _():
                drain(some, pbound.at[m])

            @pl.when(jnp.logical_not(skip))
            def _():
                drain(some, pfsend.at[m])

    gather_nodes(qb, 1, 3)
    drain(gw_hbm.at[pl.ds(0, (nn - 1) * rp)], arr.at[2])
    drain(gb_hbm.at[pl.ds(0, nn - 1)], arr.at[6])
    for k, (g, q) in ((0, (gt, qt)), (3, (gb, qb))):
        drain(g.at[pl.ds(0, nn - 1)], ars.at[k])
        drain(q.at[pl.ds(0, nf - 1)], ars.at[k + 1])
        drain(gfin.at[pl.ds(0, (nn - 1) * rp)], ars.at[k + 2])
    drain(bslot.at[pl.ds(0, nn - 1)], ars.at[6])
    for c in range(nch):
        drain(out_v.at[pl.ds(c * cr, cr)], out_sem.at[c])
    mine = gfin.at[pl.ds(0, rp)]
    drain(mine, load_sem.at[4])
    drain(bslot.at[0], load_sem.at[6])
    drain(mine, load_sem.at[5])
    drain(gw_hbm.at[pl.ds(0, (nn - 1) * rp)], arr.at[5])


def per_device(nn, nf, feats, tile_src, tile_weight, w_one, b_one, w_two, b_two, cotangent):
    fd = feats.shape[0]
    nb, neigh = tile_src.shape
    rows = nb * TILE
    hid = b_one.shape[0]
    features = w_one.shape[0]
    rp = hid // nn
    ch = min(4, nb)
    nch = nb // ch
    anyspace = pl.BlockSpec(memory_space=pl.ANY)
    vm = pl.BlockSpec(memory_space=pltpu.VMEM)
    sm = pl.BlockSpec(memory_space=pltpu.SMEM)
    dma = pltpu.SemaphoreType.DMA
    out, gw, gb = pl.pallas_call(
        functools.partial(kernel, nn, nf, nb, neigh, ch),
        out_shape=(
            jax.ShapeDtypeStruct((rows, hid), BF),
            jax.ShapeDtypeStruct((2 * hid, hid), BF),
            jax.ShapeDtypeStruct((nn, 8, hid), F32),
        ),
        in_specs=[anyspace, sm, anyspace, anyspace, vm, anyspace, vm, anyspace],
        out_specs=(anyspace,) * 3,
        scratch_shapes=[
            pltpu.VMEM((features, 3 * rows), BF),
            pltpu.VMEM((fd, nf * rows), BF),
            pltpu.VMEM((3 * nb, features // 2, TILE), BF),
            pltpu.VMEM((3 * nb, features // 2, TILE), BF),
            pltpu.VMEM(tile_weight.shape, BF),
            pltpu.VMEM((features, 3 * rows), BF),
            pltpu.VMEM((3 * nb, TILE, hid), BF),
            pltpu.VMEM((rows, hid), BF),
            pltpu.VMEM((rows, hid), BF),
            pltpu.VMEM((hid, rows), BF),
            pltpu.VMEM(w_one.shape, BF),
            pltpu.VMEM(w_two.shape, BF),
            pltpu.VMEM((rows, hid), BF),
            pltpu.VMEM((nn, rp, hid), BF),
            pltpu.VMEM((nn, rp, hid), BF),
            pltpu.VMEM((nf, rp + 8, hid), F32),
            pltpu.VMEM((nn, rp, hid), BF),
            pltpu.VMEM((nn, rp, hid), BF),
            pltpu.VMEM((nf, rp, hid), F32),
            pltpu.VMEM((2 * hid, hid), BF),
            pltpu.VMEM((nn, 8, hid), F32),
            pltpu.VMEM((hid, hid), F32),
            pltpu.SMEM((nb, neigh), jnp.int32),
            dma((7,)), dma((1,)), dma((nf,)), dma((2,)), dma((2,)), dma((1,)), dma((2,)),
            dma((2 * nch + 1,)), dma((2 * nch + 1,)), dma((2 * nch + 1,)), dma((2 * nch + 1,)), dma((2 * nch + 1,)),
            dma((7,)), dma((7,)), dma((nch,)),
        ],
        compiler_params=pltpu.CompilerParams(
            collective_id=0, has_side_effects=True, vmem_limit_bytes=56 * 2**20),
        name="sage",
    )(feats, tile_src, tile_weight, w_one, b_one.reshape(1, hid), w_two, b_two.reshape(1, hid), cotangent)
    out, gw, gb = pl.pallas_call(
        hand_over,
        out_shape=(
            jax.ShapeDtypeStruct((rows, hid), BF),
            jax.ShapeDtypeStruct((2 * hid, hid), F32),
            jax.ShapeDtypeStruct((1, hid), F32),
        ),
        in_specs=[vm] * 3,
        out_specs=(vm,) * 3,
        name="hand_over",
    )(out, gw, gb)
    return out, gw, gb.reshape(hid)


def solution(mesh):
    nn, nf = mesh.shape["nodes"], mesh.shape["feat"]
    return jax.shard_map(
        functools.partial(per_device, nn, nf),
        mesh=mesh,
        in_specs=(
            P("feat", "nodes"),
            P(("nodes", "feat"), None),
            P(("nodes", "feat"), None, None, None),
            P(),
            P(),
            P(),
            P(),
            P(("nodes", "feat"), None),
        ),
        out_specs=(P(("nodes", "feat"), None), P(), P()),
        check_vma=False,
    )
```

```python
import functools

import jax
import jax.numpy as jnp
from jax import lax
from jax.experimental import pallas as pl
from jax.experimental.pallas import tpu as pltpu
from jax.sharding import PartitionSpec as P

BF = jnp.bfloat16
F32 = jnp.float32
TILE = 128
MESH = pl.DeviceIdType.MESH


def remote(src, dst, send_sem, recv_sem, node, feat):
    return pltpu.make_async_remote_copy(
        src_ref=src, dst_ref=dst, send_sem=send_sem, recv_sem=recv_sem,
        device_id=(node, feat), device_id_type=MESH)


def drain(ref, sem):
    pltpu.make_async_copy(ref, ref, sem).wait()


def dot(a, b):
    return lax.dot_general(a, b, (((1,), (0,)), ((), ())), preferred_element_type=F32)


def dot_nt(a, b):
    return lax.dot_general(a, b, (((1,), (1,)), ((), ())), preferred_element_type=F32)


def hand_over(out, gw, gb, out_copy, gw_wide, gb_sum, out_v, gw_v, gb_v, wide_v, sum_v, came, left):
    parts = came.shape[0] - 2
    size = out.shape[0] // parts
    here = [pltpu.make_async_copy(out.at[pl.ds(i * size, size)], out_v.at[pl.ds(i * size, size)], came.at[i])
            for i in range(parts)]
    there = [pltpu.make_async_copy(out_v.at[pl.ds(i * size, size)], out_copy.at[pl.ds(i * size, size)], left.at[i])
             for i in range(parts)]
    here += [pltpu.make_async_copy(gw, gw_v, came.at[parts]), pltpu.make_async_copy(gb, gb_v, came.at[parts + 1])]
    there += [pltpu.make_async_copy(wide_v, gw_wide, left.at[parts]),
              pltpu.make_async_copy(sum_v, gb_sum, left.at[parts + 1])]
    for i in (parts, *range(parts), parts + 1):
        here[i].start()
    here[parts].wait()
    wide_v[...] = gw_v[...].astype(F32)
    there[parts].start()
    for i in range(parts):
        here[i].wait()
        there[i].start()
    here[parts + 1].wait()
    tot = gb_v[0]
    for i in range(1, gb.shape[0]):
        tot = tot + gb_v[i]
    sum_v[...] = jnp.sum(tot, axis=0, keepdims=True)
    there[parts + 1].start()
    for copy in there:
        copy.wait()


def kernel(nn, nf, nb, neigh, chunk_blocks,
           feats, src, a_hbm, w1_hbm, b1, w2_hbm, b2, cot_hbm,
           out_hbm, gw_hbm, gb_hbm,
           ft, zb, fa, fb, a_v, pt, hn, mn, cot_v, cot_t, w1_v, w2_v, out_v,
           gt, rt, qt, gb, rb, qb, gfin, bslot, g_acc, loc,
           load_sem, zsend, zrecv, fsend, fedge, fextra, frecv, psend, pbound, pfsend, pdir, pfwd,
           ars, arr, out_sem):
    fd = feats.shape[0]
    rows = nb * TILE
    hid = b1.shape[1]
    rp = hid // nn
    ch = chunk_blocks
    nch = nb // ch
    cr = ch * TILE
    hc = ch // 2
    start = [(0, hc), (hc, hc)]
    plan = (start + [(c * ch, ch) for c in range(1, nch)],
            start + [(c * ch, ch) for c in range(1, nch - 1)] + [(nb - ch, hc), (nb - hc, hc)])
    first_b = len(plan[0])
    last = len(plan[1]) - 1
    straight_set = ((1, last),)
    n = lax.axis_index("nodes")
    f = lax.axis_index("feat")
    z = lax.rem(f, 2)
    n_next = lax.rem(n + 1, nn)
    n_prev = lax.rem(n + nn - 1, nn)

    loads = [
        pltpu.make_async_copy(w1_hbm, w1_v, load_sem.at[0]),
        pltpu.make_async_copy(cot_hbm, cot_v, load_sem.at[1]),
        pltpu.make_async_copy(a_hbm, a_v, load_sem.at[2]),
        pltpu.make_async_copy(w2_hbm, w2_v, load_sem.at[3]),
    ]
    for load in loads:
        load.start()

    barrier = pltpu.get_barrier_semaphore()

    def greet(node, feat):
        pl.semaphore_signal(barrier, inc=1, device_id=(node, feat), device_id_type=MESH)

    for d in range(1, nf):
        greet(n, lax.rem(f + d, nf))
    for d in range(1, nn):
        greet(lax.rem(n + d, nn), f)

    @pl.when(f == 0)
    def _():
        for g in range(nf):
            greet(n_prev, jnp.int32(g))

    @pl.when(f == nf - 1)
    def _():
        for g in range(nf):
            greet(n_next, jnp.int32(g))

    pl.semaphore_wait(barrier, nf + nn)

    partner = f + 1 - 2 * z
    half = nf * fd // 2
    row_own = (f // 2) * fd + z * half
    row_other = (f // 2) * fd + (1 - z) * half

    def columns(j):
        return pl.ds(pl.multiple_of(j * rows, rows), rows)

    far_first = sorted(range(nf), key=lambda t: (abs(t - nf // 2), t))
    for t in far_first:
        j = lax.rem(partner + t, nf)
        remote(feats.at[:, columns(j)], zb.at[:, columns(j)], zsend.at[0], zrecv.at[t], n, partner).start()

    cross = lax.rem(n + f, 2) == 1

    def spread(t, source, row, h):
        j = lax.rem(f + t, nf)
        s = source.at[:, columns(j)]

        def to(part):
            return ft.at[pl.ds(pl.multiple_of(row, fd), fd), pl.ds(part * rows, rows)]

        def keep(part):
            pltpu.make_async_copy(s, to(part), frecv.at[h]).start()

        def send(part, node, feat):
            remote(s, to(part), fsend.at[h], frecv.at[h], node, feat).start()

        def over(part, node, feat, sem, recv):
            remote(s, to(part), sem, frecv.at[recv], node, jnp.int32(feat)).start()

        if t % 2 == 0:
            if t == 0:
                keep(1)
            else:
                send(1, n, j)
            if h == 0:
                pl.when(jnp.logical_and(j == nf - 1, lax.rem(n, 2) == 1))(
                    lambda: over(0, n_next, 0, fextra.at[0], 1))
                pl.when(jnp.logical_and(j == 0, lax.rem(n, 2) == 0))(
                    lambda: over(2, n_prev, nf - 1, fextra.at[0], 1))
            return
        ours = True if h == 0 else jnp.logical_not(cross)
        for part, at_edge, step, node, feat, own in ((0, j == nf - 1, 1, n_next, 0, nf - 1),
                                                     (2, j == 0, nf - 1, n_prev, nf - 1, 1)):
            pl.when(jnp.logical_and(at_edge, ours))(
                functools.partial(over, part, node, feat, fedge.at[h], h))
            inside = functools.partial(keep, part) if t == own else functools.partial(
                send, part, n, lax.rem(j + step, nf))
            pl.when(jnp.logical_not(at_edge))(inside)

    for t in far_first:
        spread(t, feats, row_own, 0)

    def pass_on(t):
        drain(zb.at[:, pl.ds(0, rows)], zrecv.at[t])
        spread(t, zb, row_other, 1)

    loads[1].wait()

    def cot_step(i, acc):
        base = pl.multiple_of(i * TILE, TILE)
        c = cot_v[pl.ds(base, TILE), :]
        cot_t[:, pl.ds(base, TILE)] = c.T
        return acc + c.astype(F32).reshape(TILE // 8, 8, hid).sum(0)

    bias_part = lax.fori_loop(0, nb // 2, cot_step, jnp.zeros((8, hid), F32))
    pass_on(far_first[0])
    bias_part = lax.fori_loop(nb // 2, nb, cot_step, bias_part)
    for t in far_first[1:-2]:
        pass_on(t)

    first = (n * nf + f - 1) * nb
    total = nn * nf * nb

    def locate(b, carry):
        for k in range(neigh):
            s = src[b, k] - first
            s = jnp.where(s >= total, s - total, s)
            s = jnp.where(s < 0, s + total, s)
            loc[b, k] = jnp.minimum(s, 3 * nb - 1)
        return carry

    def pick(table, b, k):
        return table[loc[b, k]]

    def pair(b, k):
        return jnp.concatenate([a_v[b, k], a_v[b, k + 1]], axis=1)

    bound_next = jnp.logical_and(f == nf - 1, lax.rem(n, 2) == 1)
    bound_prev = jnp.logical_and(f == 0, lax.rem(n, 2) == 0)
    out_base = z * (2 * nb)
    in_base = (2 - 2 * z) * nb

    def at_cols(row, block, count):
        return pt.at[pl.ds(pl.multiple_of(row, half), half),
                     pl.ds(pl.multiple_of(block * TILE, count * TILE), count * TILE)]

    def arrange(table, row, h):
        drain(ft.at[pl.ds(0, half)], frecv.at[h])

        def step(i, carry):
            table[i] = ft[pl.ds(pl.multiple_of(row, half), half), pl.ds(pl.multiple_of(i * TILE, TILE), TILE)]
            return carry

        lax.fori_loop(0, 3 * nb, step, 0, unroll=4)

    direct_f = lax.rem(f + jnp.where(z == 0, nf - 1, 1), nf)
    direct_n = jnp.where(f == 0, n_prev, jnp.where(f == nf - 1, n_next, n))
    direct_base = (2 - 2 * z) * nb

    def one_chunk(table, row, h, m, block, count, straight=False):
        for i in range(count):
            b = block + i
            acc = None
            for k in range(0, neigh, 2):
                p = dot_nt(jnp.concatenate([pick(table, b, k), pick(table, b, k + 1)], axis=1), pair(b, k))
                acc = p if acc is None else acc + p
            pt[pl.ds(pl.multiple_of(row, half), half),
               pl.ds(pl.multiple_of((nb + b) * TILE, TILE), TILE)] = acc.astype(BF)
        own = at_cols(row, nb + block, count)
        remote(own, at_cols(row, out_base + block, count), psend.at[m], pdir.at[m], n, partner).start()

        def direct():
            remote(own, at_cols(row, direct_base + block, count), pbound.at[m], pfwd.at[m],
                   direct_n, direct_f).start()

        if straight:
            direct()
        else:
            pl.when(jnp.logical_or(bound_next, bound_prev))(direct)

    skip = jnp.logical_or(jnp.logical_and(f == nf - 2, lax.rem(n, 2) == 1),
                          jnp.logical_and(f == 1, lax.rem(n, 2) == 0))
    fwd_f = lax.rem(f + jnp.where(z == 0, 2, nf - 2), nf)
    fwd_n = jnp.where(f == nf - 2, n_next, jnp.where(f == 1, n_prev, n))

    def forward(h, c):
        m = h * first_b + c
        block, count = plan[h][c]
        row = (1 - z) * half if h == 0 else z * half
        came = at_cols(row, in_base + block, count)
        drain(came, pdir.at[m])
        if (h, c) in straight_set:
            return

        @pl.when(jnp.logical_not(skip))
        def _():
            remote(came, at_cols(row, out_base + block, count), pfsend.at[m], pfwd.at[m], fwd_n, fwd_f).start()

    lax.fori_loop(0, nb, locate, 0)
    arrange(fa, z * half, 0)
    loads[2].wait()
    row_a, row_b = z * half, (1 - z) * half
    one_chunk(fa, row_a, 0, 0, *plan[0][0])
    pass_on(far_first[-2])
    one_chunk(fa, row_a, 0, 1, *plan[0][1])
    pass_on(far_first[-1])
    lax.fori_loop(1, nch, lambda c, u: (one_chunk(fa, row_a, 0, 1 + c, c * ch, ch), u)[1], 0)
    arrange(fb, row_b, 1)
    for c in range(first_b):
        forward(0, c)
    for c in range(2):
        one_chunk(fb, row_b, 1, first_b + c, *plan[1][c])
    if nch > 2:
        lax.fori_loop(1, nch - 1, lambda c, u: (one_chunk(fb, row_b, 1, first_b + 1 + c, c * ch, ch), u)[1], 0)
    for c in (last - 1, last):
        one_chunk(fb, row_b, 1, first_b + c, *plan[1][c], (1, c) in straight_set)

    loads[0].wait()
    order = [g * fd for g in range(0, nf, 2)] + [g * fd for g in range(1, nf, 2)]
    w_cat = jnp.concatenate(
        [w1_v[g:g + fd, :hid] for g in order] + [w1_v[g:g + fd, hid:] for g in order], axis=0)
    bias_one = b1[...]

    def hidden(base, count):
        def step(i, carry):
            at = pl.ds(base + i * 2, 2)
            cols = pl.ds(pl.multiple_of((base + i * 2) * TILE, 2 * TILE), 2 * TILE)
            v = dot(jnp.concatenate([ft[:, cols], pt[:, cols]], axis=0).T, w_cat) + bias_one
            hn[at] = jnp.maximum(v, 0.0).astype(BF).reshape(2, TILE, hid)
            return carry

        lax.fori_loop(0, count // 2, step, 0, unroll=min(4, count // 2))

    def pieces(g, grad):
        for i in range(nn):
            g[i] = grad[i * rp:(i + 1) * rp, :].astype(BF)

    def scatter_nodes(g, r, k):
        for d in range(1, nn):
            dn = lax.rem(n + d, nn)
            remote(g.at[dn], r.at[n], ars.at[k], arr.at[k], dn, f).start()
        r[n] = g[n]

    def share_feat(g, r, q, k, extra):
        drain(r.at[pl.ds(0, nn - 1)], arr.at[k])
        tot = r[0].astype(F32)
        for i in range(1, nn):
            tot = tot + r[i].astype(F32)
        q[f, 0:rp, :] = tot
        if extra is not None:
            q[f, rp:, :] = extra
        for d in range(1, nf):
            remote(q.at[f], q.at[f], ars.at[k + 1], arr.at[k + 1], n, lax.rem(f + d, nf)).start()

    def gather_nodes(q, half, k):
        drain(q.at[pl.ds(0, nf - 1)], arr.at[k + 1])
        tot = q[0]
        for i in range(1, nf):
            tot = tot + q[i]
        at = pl.ds(pl.multiple_of(half * hid + n * rp, rp), rp)
        gfin[at, :] = tot[0:rp, :].astype(BF)
        for d in range(1, nn):
            remote(gfin.at[at], gw_hbm.at[at], ars.at[k + 2], arr.at[k + 2], lax.rem(n + d, nn), f).start()
        pltpu.make_async_copy(gfin.at[at], gw_hbm.at[at], load_sem.at[4 + half]).start()
        if half == 0:
            bslot[n] = tot[rp:, :]
            for d in range(1, nn):
                remote(bslot.at[n], gb_hbm.at[n], ars.at[6], arr.at[6], lax.rem(n + d, nn), f).start()
            pltpu.make_async_copy(bslot.at[n], gb_hbm.at[n], load_sem.at[6]).start()

    def halo(c, seen):
        block, count = plan[1][c]
        for m in range(seen, first_b):
            if plan[0][m][0] < block + count:
                drain(at_cols(0, *plan[0][m]), pfwd.at[m])
                seen = m + 1
        drain(at_cols(0, block, count), pfwd.at[first_b + c])
        hidden(out_base + block, count)
        return seen

    forward(1, 0)
    forward(1, 1)
    hidden(nb, nb)
    if last > 3:
        forward(1, 2)
    pieces(gt, dot(cot_t[...], hn[nb:2 * nb].reshape(rows, hid)).T)
    for c in range(3 if last > 3 else 2, last - 1):
        forward(1, c)
    hidden(in_base, nb // 2)
    forward(1, last - 1)
    scatter_nodes(gt, rt, 0)
    forward(1, last)
    hidden(in_base + nb // 2, nb // 2)
    seen = 0
    for c in range(last + 1):
        seen = halo(c, seen)

    def two_chunk(c, carry):
        turned = []
        for i in range(ch):
            b = c * ch + i
            at = pl.ds(pl.multiple_of(b * TILE, TILE), TILE)
            acc = None
            for k in range(0, neigh, 2):
                p = dot(pair(b, k), jnp.concatenate([pick(hn, b, k), pick(hn, b, k + 1)], axis=0))
                acc = p if acc is None else acc + p
            mixed = acc.astype(BF)
            mn[at, :] = mixed
            turned.append(mixed.T)
        at = pl.ds(pl.multiple_of(c * cr, cr), cr)
        g_acc[...] += dot(jnp.concatenate(turned, axis=1), cot_v[at, :])
        return carry

    g_acc[...] = jnp.zeros_like(g_acc)
    lax.fori_loop(0, nch - 1, two_chunk, 0)
    share_feat(gt, rt, qt, 0, bias_part)
    two_chunk(nch - 1, 0)
    pieces(gb, g_acc[...])
    scatter_nodes(gb, rb, 3)

    loads[3].wait()
    bias_two = b2[...]

    def out_chunk(c, carry):
        at = pl.ds(pl.multiple_of(c * cr, cr), cr)
        own = hn[pl.ds(nb + c * ch, ch)].reshape(cr, hid)
        both = jnp.concatenate([own, mn[at, :]], axis=1)
        out_v[at, :] = (dot(both, w2_v[...]) + bias_two).astype(BF)
        pltpu.make_async_copy(out_v.at[at], out_hbm.at[at], out_sem.at[c]).start()
        return carry

    lax.fori_loop(0, nch, out_chunk, 0)

    share_feat(gb, rb, qb, 3, None)
    gather_nodes(qt, 0, 0)

    drain(zb, zsend.at[0])
    piece = ft.at[pl.ds(0, fd), pl.ds(0, rows)]
    ends = jnp.logical_or(f == 0, f == nf - 1)
    for h in range(2):
        @pl.when(ends)
        def _():
            drain(ft.at[pl.ds(0, (nf + 1) * fd // 3), :], fsend.at[h])

        @pl.when(jnp.logical_not(ends))
        def _():
            drain(zb, fsend.at[h])

    drain(piece, fedge.at[0])

    @pl.when(jnp.logical_not(cross))
    def _():
        drain(piece, fedge.at[1])
        drain(piece, fextra.at[0])

    for h in range(2):
        for c in range(len(plan[h])):
            m = h * first_b + c
            some = at_cols(0, *plan[h][c])
            drain(some, psend.at[m])
            if (h, c) in straight_set:
                drain(some, pbound.at[m])
                continue

            @pl.when(jnp.logical_or(bound_next, bound_prev))
            def _():
                drain(some, pbound.at[m])

            @pl.when(jnp.logical_not(skip))
            def _():
                drain(some, pfsend.at[m])

    gather_nodes(qb, 1, 3)
    drain(gw_hbm.at[pl.ds(0, (nn - 1) * rp)], arr.at[2])
    drain(gb_hbm.at[pl.ds(0, nn - 1)], arr.at[6])
    for k, (g, q) in ((0, (gt, qt)), (3, (gb, qb))):
        drain(g.at[pl.ds(0, nn - 1)], ars.at[k])
        drain(q.at[pl.ds(0, nf - 1)], ars.at[k + 1])
        drain(gfin.at[pl.ds(0, (nn - 1) * rp)], ars.at[k + 2])
    drain(bslot.at[pl.ds(0, nn - 1)], ars.at[6])
    for c in range(nch):
        drain(out_v.at[pl.ds(c * cr, cr)], out_sem.at[c])
    mine = gfin.at[pl.ds(0, rp)]
    drain(mine, load_sem.at[4])
    drain(bslot.at[0], load_sem.at[6])
    drain(mine, load_sem.at[5])
    drain(gw_hbm.at[pl.ds(0, (nn - 1) * rp)], arr.at[5])


def per_device(nn, nf, feats, tile_src, tile_weight, w_one, b_one, w_two, b_two, cotangent):
    fd = feats.shape[0]
    nb, neigh = tile_src.shape
    rows = nb * TILE
    hid = b_one.shape[0]
    features = w_one.shape[0]
    rp = hid // nn
    ch = min(4, nb)
    nch = nb // ch
    anyspace = pl.BlockSpec(memory_space=pl.ANY)
    vm = pl.BlockSpec(memory_space=pltpu.VMEM)
    sm = pl.BlockSpec(memory_space=pltpu.SMEM)
    dma = pltpu.SemaphoreType.DMA
    out, gw, gb = pl.pallas_call(
        functools.partial(kernel, nn, nf, nb, neigh, ch),
        out_shape=(
            jax.ShapeDtypeStruct((rows, hid), BF),
            jax.ShapeDtypeStruct((2 * hid, hid), BF),
            jax.ShapeDtypeStruct((nn, 8, hid), F32),
        ),
        in_specs=[anyspace, sm, anyspace, anyspace, vm, anyspace, vm, anyspace],
        out_specs=(anyspace,) * 3,
        scratch_shapes=[
            pltpu.VMEM((features, 3 * rows), BF),
            pltpu.VMEM((fd, nf * rows), BF),
            pltpu.VMEM((3 * nb, features // 2, TILE), BF),
            pltpu.VMEM((3 * nb, features // 2, TILE), BF),
            pltpu.VMEM(tile_weight.shape, BF),
            pltpu.VMEM((features, 3 * rows), BF),
            pltpu.VMEM((3 * nb, TILE, hid), BF),
            pltpu.VMEM((rows, hid), BF),
            pltpu.VMEM((rows, hid), BF),
            pltpu.VMEM((hid, rows), BF),
            pltpu.VMEM(w_one.shape, BF),
            pltpu.VMEM(w_two.shape, BF),
            pltpu.VMEM((rows, hid), BF),
            pltpu.VMEM((nn, rp, hid), BF),
            pltpu.VMEM((nn, rp, hid), BF),
            pltpu.VMEM((nf, rp + 8, hid), F32),
            pltpu.VMEM((nn, rp, hid), BF),
            pltpu.VMEM((nn, rp, hid), BF),
            pltpu.VMEM((nf, rp, hid), F32),
            pltpu.VMEM((2 * hid, hid), BF),
            pltpu.VMEM((nn, 8, hid), F32),
            pltpu.VMEM((hid, hid), F32),
            pltpu.SMEM((nb, neigh), jnp.int32),
            dma((7,)), dma((1,)), dma((nf,)), dma((2,)), dma((2,)), dma((1,)), dma((2,)),
            dma((2 * nch + 3,)), dma((2 * nch + 3,)), dma((2 * nch + 3,)), dma((2 * nch + 3,)), dma((2 * nch + 3,)),
            dma((7,)), dma((7,)), dma((nch,)),
        ],
        compiler_params=pltpu.CompilerParams(
            collective_id=0, has_side_effects=True, vmem_limit_bytes=56 * 2**20),
        name="sage",
    )(feats, tile_src, tile_weight, w_one, b_one.reshape(1, hid), w_two, b_two.reshape(1, hid), cotangent)
    out, gw, gb = pl.pallas_call(
        hand_over,
        out_shape=(
            jax.ShapeDtypeStruct((rows, hid), BF),
            jax.ShapeDtypeStruct((2 * hid, hid), F32),
            jax.ShapeDtypeStruct((1, hid), F32),
        ),
        in_specs=[anyspace] * 3,
        out_specs=(anyspace,) * 3,
        scratch_shapes=[
            pltpu.VMEM((rows, hid), BF),
            pltpu.VMEM((2 * hid, hid), BF),
            pltpu.VMEM((nn, 8, hid), F32),
            pltpu.VMEM((2 * hid, hid), F32),
            pltpu.VMEM((1, hid), F32),
            dma((4,)), dma((4,)),
        ],
        name="hand_over",
    )(out, gw, gb)
    return out, gw, gb.reshape(hid)


def solution(mesh):
    nn, nf = mesh.shape["nodes"], mesh.shape["feat"]
    return jax.shard_map(
        functools.partial(per_device, nn, nf),
        mesh=mesh,
        in_specs=(
            P("feat", "nodes"),
            P(("nodes", "feat"), None),
            P(("nodes", "feat"), None, None, None),
            P(),
            P(),
            P(),
            P(),
            P(("nodes", "feat"), None),
        ),
        out_specs=(P(("nodes", "feat"), None), P(), P()),
        check_vma=False,
    )
```

```python
import functools

import jax
import jax.numpy as jnp
from jax import lax
from jax.experimental import pallas as pl
from jax.experimental.pallas import tpu as pltpu
from jax.sharding import PartitionSpec as P

BF = jnp.bfloat16
F32 = jnp.float32
TILE = 128
MESH = pl.DeviceIdType.MESH


def remote(src, dst, send_sem, recv_sem, node, feat):
    return pltpu.make_async_remote_copy(
        src_ref=src, dst_ref=dst, send_sem=send_sem, recv_sem=recv_sem,
        device_id=(node, feat), device_id_type=MESH)


def drain(ref, sem):
    pltpu.make_async_copy(ref, ref, sem).wait()


def dot(a, b):
    return lax.dot_general(a, b, (((1,), (0,)), ((), ())), preferred_element_type=F32)


def dot_nt(a, b):
    return lax.dot_general(a, b, (((1,), (1,)), ((), ())), preferred_element_type=F32)


def hand_over(out, gw, gb, out_copy, gw_wide, gb_sum, out_v, gw_v, gb_v, wide_v, sum_v, came, left):
    parts = came.shape[0] - 2
    size = out.shape[0] // parts
    here = [pltpu.make_async_copy(out.at[pl.ds(i * size, size)], out_v.at[pl.ds(i * size, size)], came.at[i])
            for i in range(parts)]
    there = [pltpu.make_async_copy(out_v.at[pl.ds(i * size, size)], out_copy.at[pl.ds(i * size, size)], left.at[i])
             for i in range(parts)]
    here += [pltpu.make_async_copy(gw, gw_v, came.at[parts]), pltpu.make_async_copy(gb, gb_v, came.at[parts + 1])]
    there += [pltpu.make_async_copy(wide_v, gw_wide, left.at[parts]),
              pltpu.make_async_copy(sum_v, gb_sum, left.at[parts + 1])]
    for i in (parts, *range(parts), parts + 1):
        here[i].start()
    here[parts].wait()
    wide_v[...] = gw_v[...].astype(F32)
    there[parts].start()
    for i in range(parts):
        here[i].wait()
        there[i].start()
    here[parts + 1].wait()
    tot = gb_v[0]
    for i in range(1, gb.shape[0]):
        tot = tot + gb_v[i]
    sum_v[...] = jnp.sum(tot, axis=0, keepdims=True)
    there[parts + 1].start()
    for copy in there:
        copy.wait()


def kernel(nn, nf, nb, neigh, chunk_blocks,
           feats, src, a_hbm, w1_hbm, b1, w2_hbm, b2, cot_hbm,
           out_hbm, gw_hbm, gb_hbm,
           ft, zb, fa, fb, a_v, pt, hn, mn, cot_v, cot_t, w1_v, w2_v, out_v,
           gt, rt, qt, gb, rb, qb, gfin, bslot, g_acc, loc,
           load_sem, zsend, zrecv, fsend, fedge, fextra, frecv, psend, pbound, pfsend, pdir, pfwd,
           ars, arr, out_sem):
    fd = feats.shape[0]
    rows = nb * TILE
    hid = b1.shape[1]
    rp = hid // nn
    ch = chunk_blocks
    nch = nb // ch
    cr = ch * TILE
    hc = ch // 2
    start = [(0, hc), (hc, hc)]
    plan = (start + [(c * ch, ch) for c in range(1, nch)],
            start + [(c * ch, ch) for c in range(1, nch - 1)] + [(nb - ch, hc), (nb - hc, hc)])
    first_b = len(plan[0])
    last = len(plan[1]) - 1
    straight_set = ((1, last),)
    n = lax.axis_index("nodes")
    f = lax.axis_index("feat")
    z = lax.rem(f, 2)
    n_next = lax.rem(n + 1, nn)
    n_prev = lax.rem(n + nn - 1, nn)

    loads = [
        pltpu.make_async_copy(w1_hbm, w1_v, load_sem.at[0]),
        pltpu.make_async_copy(cot_hbm, cot_v, load_sem.at[1]),
        pltpu.make_async_copy(a_hbm, a_v, load_sem.at[2]),
        pltpu.make_async_copy(w2_hbm, w2_v, load_sem.at[3]),
    ]
    for load in loads:
        load.start()

    barrier = pltpu.get_barrier_semaphore()

    def greet(node, feat):
        pl.semaphore_signal(barrier, inc=1, device_id=(node, feat), device_id_type=MESH)

    for d in range(1, nf):
        greet(n, lax.rem(f + d, nf))
    for d in range(1, nn):
        greet(lax.rem(n + d, nn), f)

    @pl.when(f == 0)
    def _():
        for g in range(nf):
            greet(n_prev, jnp.int32(g))

    @pl.when(f == nf - 1)
    def _():
        for g in range(nf):
            greet(n_next, jnp.int32(g))

    pl.semaphore_wait(barrier, nf + nn)

    partner = f + 1 - 2 * z
    half = nf * fd // 2
    row_own = (f // 2) * fd + z * half
    row_other = (f // 2) * fd + (1 - z) * half

    def columns(j):
        return pl.ds(pl.multiple_of(j * rows, rows), rows)

    far_first = sorted(range(nf), key=lambda t: (abs(t - nf // 2), t))
    for t in far_first:
        j = lax.rem(partner + t, nf)
        remote(feats.at[:, columns(j)], zb.at[:, columns(j)], zsend.at[0], zrecv.at[t], n, partner).start()

    cross = lax.rem(n + f, 2) == 1

    def spread(t, source, row, h):
        j = lax.rem(f + t, nf)
        s = source.at[:, columns(j)]

        def to(part):
            return ft.at[pl.ds(pl.multiple_of(row, fd), fd), pl.ds(part * rows, rows)]

        def keep(part):
            pltpu.make_async_copy(s, to(part), frecv.at[h]).start()

        def send(part, node, feat):
            remote(s, to(part), fsend.at[h], frecv.at[h], node, feat).start()

        def over(part, node, feat, sem, recv):
            remote(s, to(part), sem, frecv.at[recv], node, jnp.int32(feat)).start()

        if t % 2 == 0:
            if t == 0:
                keep(1)
            else:
                send(1, n, j)
            if h == 0:
                pl.when(jnp.logical_and(j == nf - 1, lax.rem(n, 2) == 1))(
                    lambda: over(0, n_next, 0, fextra.at[0], 1))
                pl.when(jnp.logical_and(j == 0, lax.rem(n, 2) == 0))(
                    lambda: over(2, n_prev, nf - 1, fextra.at[0], 1))
            return
        ours = True if h == 0 else jnp.logical_not(cross)
        for part, at_edge, step, node, feat, own in ((0, j == nf - 1, 1, n_next, 0, nf - 1),
                                                     (2, j == 0, nf - 1, n_prev, nf - 1, 1)):
            pl.when(jnp.logical_and(at_edge, ours))(
                functools.partial(over, part, node, feat, fedge.at[h], h))
            inside = functools.partial(keep, part) if t == own else functools.partial(
                send, part, n, lax.rem(j + step, nf))
            pl.when(jnp.logical_not(at_edge))(inside)

    for t in far_first:
        spread(t, feats, row_own, 0)

    def pass_on(t):
        drain(zb.at[:, pl.ds(0, rows)], zrecv.at[t])
        spread(t, zb, row_other, 1)

    loads[1].wait()

    def cot_step(i, acc):
        base = pl.multiple_of(i * TILE, TILE)
        c = cot_v[pl.ds(base, TILE), :]
        cot_t[:, pl.ds(base, TILE)] = c.T
        return acc + c.astype(F32).reshape(TILE // 8, 8, hid).sum(0)

    bias_part = lax.fori_loop(0, nb // 2, cot_step, jnp.zeros((8, hid), F32))
    pass_on(far_first[0])
    bias_part = lax.fori_loop(nb // 2, nb, cot_step, bias_part)
    for t in far_first[1:-2]:
        pass_on(t)

    first = (n * nf + f - 1) * nb
    total = nn * nf * nb

    def locate(b, carry):
        for k in range(neigh):
            s = src[b, k] - first
            s = jnp.where(s >= total, s - total, s)
            s = jnp.where(s < 0, s + total, s)
            loc[b, k] = jnp.minimum(s, 3 * nb - 1)
        return carry

    def pick(table, b, k):
        return table[loc[b, k]]

    def pair(b, k):
        return jnp.concatenate([a_v[b, k], a_v[b, k + 1]], axis=1)

    bound_next = jnp.logical_and(f == nf - 1, lax.rem(n, 2) == 1)
    bound_prev = jnp.logical_and(f == 0, lax.rem(n, 2) == 0)
    out_base = z * (2 * nb)
    in_base = (2 - 2 * z) * nb

    def at_cols(row, block, count):
        return pt.at[pl.ds(pl.multiple_of(row, half), half),
                     pl.ds(pl.multiple_of(block * TILE, count * TILE), count * TILE)]

    def arrange(table, row, h):
        drain(ft.at[pl.ds(0, half)], frecv.at[h])

        def step(i, carry):
            table[i] = ft[pl.ds(pl.multiple_of(row, half), half), pl.ds(pl.multiple_of(i * TILE, TILE), TILE)]
            return carry

        lax.fori_loop(0, 3 * nb, step, 0, unroll=4)

    direct_f = lax.rem(f + jnp.where(z == 0, nf - 1, 1), nf)
    direct_n = jnp.where(f == 0, n_prev, jnp.where(f == nf - 1, n_next, n))
    direct_base = (2 - 2 * z) * nb

    def one_chunk(table, row, h, m, block, count, straight=False):
        for i in range(count):
            b = block + i
            acc = None
            for k in range(0, neigh, 2):
                p = dot_nt(jnp.concatenate([pick(table, b, k), pick(table, b, k + 1)], axis=1), pair(b, k))
                acc = p if acc is None else acc + p
            pt[pl.ds(pl.multiple_of(row, half), half),
               pl.ds(pl.multiple_of((nb + b) * TILE, TILE), TILE)] = acc.astype(BF)
        own = at_cols(row, nb + block, count)
        remote(own, at_cols(row, out_base + block, count), psend.at[m], pdir.at[m], n, partner).start()

        def direct():
            remote(own, at_cols(row, direct_base + block, count), pbound.at[m], pfwd.at[m],
                   direct_n, direct_f).start()

        if straight:
            direct()
        else:
            pl.when(jnp.logical_or(bound_next, bound_prev))(direct)

    skip = jnp.logical_or(jnp.logical_and(f == nf - 2, lax.rem(n, 2) == 1),
                          jnp.logical_and(f == 1, lax.rem(n, 2) == 0))
    fwd_f = lax.rem(f + jnp.where(z == 0, 2, nf - 2), nf)
    fwd_n = jnp.where(f == nf - 2, n_next, jnp.where(f == 1, n_prev, n))

    def forward(h, c):
        m = h * first_b + c
        block, count = plan[h][c]
        row = (1 - z) * half if h == 0 else z * half
        came = at_cols(row, in_base + block, count)
        drain(came, pdir.at[m])
        if (h, c) in straight_set:
            return

        @pl.when(jnp.logical_not(skip))
        def _():
            remote(came, at_cols(row, out_base + block, count), pfsend.at[m], pfwd.at[m], fwd_n, fwd_f).start()

    lax.fori_loop(0, nb, locate, 0)
    arrange(fa, z * half, 0)
    loads[2].wait()
    row_a, row_b = z * half, (1 - z) * half
    one_chunk(fa, row_a, 0, 0, *plan[0][0])
    pass_on(far_first[-2])
    one_chunk(fa, row_a, 0, 1, *plan[0][1])
    pass_on(far_first[-1])
    lax.fori_loop(1, nch, lambda c, u: (one_chunk(fa, row_a, 0, 1 + c, c * ch, ch), u)[1], 0)
    arrange(fb, row_b, 1)
    for c in range(first_b):
        forward(0, c)
    for c in range(2):
        one_chunk(fb, row_b, 1, first_b + c, *plan[1][c])
    if nch > 2:
        lax.fori_loop(1, nch - 1, lambda c, u: (one_chunk(fb, row_b, 1, first_b + 1 + c, c * ch, ch), u)[1], 0)
    for c in (last - 1, last):
        one_chunk(fb, row_b, 1, first_b + c, *plan[1][c], (1, c) in straight_set)

    loads[0].wait()
    order = [g * fd for g in range(0, nf, 2)] + [g * fd for g in range(1, nf, 2)]
    w_cat = jnp.concatenate(
        [w1_v[g:g + fd, :hid] for g in order] + [w1_v[g:g + fd, hid:] for g in order], axis=0)
    bias_one = b1[...]

    def hidden(base, count):
        def step(i, carry):
            at = pl.ds(base + i * 2, 2)
            cols = pl.ds(pl.multiple_of((base + i * 2) * TILE, 2 * TILE), 2 * TILE)
            v = dot(jnp.concatenate([ft[:, cols], pt[:, cols]], axis=0).T, w_cat) + bias_one
            hn[at] = jnp.maximum(v, 0.0).astype(BF).reshape(2, TILE, hid)
            return carry

        lax.fori_loop(0, count // 2, step, 0, unroll=min(4, count // 2))

    def pieces(g, grad):
        for i in range(nn):
            g[i] = grad[i * rp:(i + 1) * rp, :].astype(BF)

    def scatter_nodes(g, r, k):
        for d in range(1, nn):
            dn = lax.rem(n + d, nn)
            remote(g.at[dn], r.at[n], ars.at[k], arr.at[k], dn, f).start()
        r[n] = g[n]

    def share_feat(g, r, q, k, extra):
        drain(r.at[pl.ds(0, nn - 1)], arr.at[k])
        tot = r[0].astype(F32)
        for i in range(1, nn):
            tot = tot + r[i].astype(F32)
        q[f, 0:rp, :] = tot
        if extra is not None:
            q[f, rp:, :] = extra
        for d in range(1, nf):
            remote(q.at[f], q.at[f], ars.at[k + 1], arr.at[k + 1], n, lax.rem(f + d, nf)).start()

    def gather_nodes(q, half, k):
        drain(q.at[pl.ds(0, nf - 1)], arr.at[k + 1])
        tot = q[0]
        for i in range(1, nf):
            tot = tot + q[i]
        at = pl.ds(pl.multiple_of(half * hid + n * rp, rp), rp)
        gfin[at, :] = tot[0:rp, :].astype(BF)
        for d in range(1, nn):
            remote(gfin.at[at], gw_hbm.at[at], ars.at[k + 2], arr.at[k + 2], lax.rem(n + d, nn), f).start()
        pltpu.make_async_copy(gfin.at[at], gw_hbm.at[at], load_sem.at[4 + half]).start()
        if half == 0:
            bslot[n] = tot[rp:, :]
            for d in range(1, nn):
                remote(bslot.at[n], gb_hbm.at[n], ars.at[6], arr.at[6], lax.rem(n + d, nn), f).start()
            pltpu.make_async_copy(bslot.at[n], gb_hbm.at[n], load_sem.at[6]).start()

    def halo(c, seen):
        block, count = plan[1][c]
        for m in range(seen, first_b):
            if plan[0][m][0] < block + count:
                drain(at_cols(0, *plan[0][m]), pfwd.at[m])
                seen = m + 1
        drain(at_cols(0, block, count), pfwd.at[first_b + c])
        hidden(out_base + block, count)
        return seen

    forward(1, 0)
    forward(1, 1)
    hidden(nb, nb)
    if last > 3:
        forward(1, 2)
    pieces(gt, dot(cot_t[...], hn[nb:2 * nb].reshape(rows, hid)).T)
    for c in range(3 if last > 3 else 2, last - 1):
        forward(1, c)
    hidden(in_base, nb // 2)
    forward(1, last - 1)
    scatter_nodes(gt, rt, 0)
    forward(1, last)
    hidden(in_base + nb // 2, nb // 2)
    seen = 0
    for c in range(last + 1):
        seen = halo(c, seen)

    def two_chunk(c, carry):
        turned = []
        for i in range(ch):
            b = c * ch + i
            at = pl.ds(pl.multiple_of(b * TILE, TILE), TILE)
            acc = None
            for k in range(0, neigh, 2):
                p = dot(pair(b, k), jnp.concatenate([pick(hn, b, k), pick(hn, b, k + 1)], axis=0))
                acc = p if acc is None else acc + p
            mixed = acc.astype(BF)
            mn[at, :] = mixed
            turned.append(mixed.T)
        at = pl.ds(pl.multiple_of(c * cr, cr), cr)
        g_acc[...] += dot(jnp.concatenate(turned, axis=1), cot_v[at, :])
        return carry

    g_acc[...] = jnp.zeros_like(g_acc)
    lax.fori_loop(0, nch, two_chunk, 0, unroll=2)
    pieces(gb, g_acc[...])
    scatter_nodes(gb, rb, 3)
    share_feat(gt, rt, qt, 0, bias_part)

    loads[3].wait()
    bias_two = b2[...]

    def out_chunk(c, carry):
        at = pl.ds(pl.multiple_of(c * cr, cr), cr)
        own = hn[pl.ds(nb + c * ch, ch)].reshape(cr, hid)
        both = jnp.concatenate([own, mn[at, :]], axis=1)
        out_v[at, :] = (dot(both, w2_v[...]) + bias_two).astype(BF)
        pltpu.make_async_copy(out_v.at[at], out_hbm.at[at], out_sem.at[c]).start()
        return carry

    lax.fori_loop(0, nch, out_chunk, 0)

    share_feat(gb, rb, qb, 3, None)
    gather_nodes(qt, 0, 0)

    drain(zb, zsend.at[0])
    piece = ft.at[pl.ds(0, fd), pl.ds(0, rows)]
    ends = jnp.logical_or(f == 0, f == nf - 1)
    for h in range(2):
        @pl.when(ends)
        def _():
            drain(ft.at[pl.ds(0, (nf + 1) * fd // 3), :], fsend.at[h])

        @pl.when(jnp.logical_not(ends))
        def _():
            drain(zb, fsend.at[h])

    drain(piece, fedge.at[0])

    @pl.when(jnp.logical_not(cross))
    def _():
        drain(piece, fedge.at[1])
        drain(piece, fextra.at[0])

    for h in range(2):
        for c in range(len(plan[h])):
            m = h * first_b + c
            some = at_cols(0, *plan[h][c])
            drain(some, psend.at[m])
            if (h, c) in straight_set:
                drain(some, pbound.at[m])
                continue

            @pl.when(jnp.logical_or(bound_next, bound_prev))
            def _():
                drain(some, pbound.at[m])

            @pl.when(jnp.logical_not(skip))
            def _():
                drain(some, pfsend.at[m])

    gather_nodes(qb, 1, 3)
    drain(gw_hbm.at[pl.ds(0, (nn - 1) * rp)], arr.at[2])
    drain(gb_hbm.at[pl.ds(0, nn - 1)], arr.at[6])
    for k, (g, q) in ((0, (gt, qt)), (3, (gb, qb))):
        drain(g.at[pl.ds(0, nn - 1)], ars.at[k])
        drain(q.at[pl.ds(0, nf - 1)], ars.at[k + 1])
        drain(gfin.at[pl.ds(0, (nn - 1) * rp)], ars.at[k + 2])
    drain(bslot.at[pl.ds(0, nn - 1)], ars.at[6])
    for c in range(nch):
        drain(out_v.at[pl.ds(c * cr, cr)], out_sem.at[c])
    mine = gfin.at[pl.ds(0, rp)]
    drain(mine, load_sem.at[4])
    drain(bslot.at[0], load_sem.at[6])
    drain(mine, load_sem.at[5])
    drain(gw_hbm.at[pl.ds(0, (nn - 1) * rp)], arr.at[5])


def per_device(nn, nf, feats, tile_src, tile_weight, w_one, b_one, w_two, b_two, cotangent):
    fd = feats.shape[0]
    nb, neigh = tile_src.shape
    rows = nb * TILE
    hid = b_one.shape[0]
    features = w_one.shape[0]
    rp = hid // nn
    ch = min(4, nb)
    nch = nb // ch
    anyspace = pl.BlockSpec(memory_space=pl.ANY)
    vm = pl.BlockSpec(memory_space=pltpu.VMEM)
    sm = pl.BlockSpec(memory_space=pltpu.SMEM)
    dma = pltpu.SemaphoreType.DMA
    out, gw, gb = pl.pallas_call(
        functools.partial(kernel, nn, nf, nb, neigh, ch),
        out_shape=(
            jax.ShapeDtypeStruct((rows, hid), BF),
            jax.ShapeDtypeStruct((2 * hid, hid), BF),
            jax.ShapeDtypeStruct((nn, 8, hid), F32),
        ),
        in_specs=[anyspace, sm, anyspace, anyspace, vm, anyspace, vm, anyspace],
        out_specs=(anyspace,) * 3,
        scratch_shapes=[
            pltpu.VMEM((features, 3 * rows), BF),
            pltpu.VMEM((fd, nf * rows), BF),
            pltpu.VMEM((3 * nb, features // 2, TILE), BF),
            pltpu.VMEM((3 * nb, features // 2, TILE), BF),
            pltpu.VMEM(tile_weight.shape, BF),
            pltpu.VMEM((features, 3 * rows), BF),
            pltpu.VMEM((3 * nb, TILE, hid), BF),
            pltpu.VMEM((rows, hid), BF),
            pltpu.VMEM((rows, hid), BF),
            pltpu.VMEM((hid, rows), BF),
            pltpu.VMEM(w_one.shape, BF),
            pltpu.VMEM(w_two.shape, BF),
            pltpu.VMEM((rows, hid), BF),
            pltpu.VMEM((nn, rp, hid), BF),
            pltpu.VMEM((nn, rp, hid), BF),
            pltpu.VMEM((nf, rp + 8, hid), F32),
            pltpu.VMEM((nn, rp, hid), BF),
            pltpu.VMEM((nn, rp, hid), BF),
            pltpu.VMEM((nf, rp, hid), F32),
            pltpu.VMEM((2 * hid, hid), BF),
            pltpu.VMEM((nn, 8, hid), F32),
            pltpu.VMEM((hid, hid), F32),
            pltpu.SMEM((nb, neigh), jnp.int32),
            dma((7,)), dma((1,)), dma((nf,)), dma((2,)), dma((2,)), dma((1,)), dma((2,)),
            dma((2 * nch + 3,)), dma((2 * nch + 3,)), dma((2 * nch + 3,)), dma((2 * nch + 3,)), dma((2 * nch + 3,)),
            dma((7,)), dma((7,)), dma((nch,)),
        ],
        compiler_params=pltpu.CompilerParams(
            collective_id=0, has_side_effects=True, vmem_limit_bytes=56 * 2**20),
        name="sage",
    )(feats, tile_src, tile_weight, w_one, b_one.reshape(1, hid), w_two, b_two.reshape(1, hid), cotangent)
    out, gw, gb = pl.pallas_call(
        hand_over,
        out_shape=(
            jax.ShapeDtypeStruct((rows, hid), BF),
            jax.ShapeDtypeStruct((2 * hid, hid), F32),
            jax.ShapeDtypeStruct((1, hid), F32),
        ),
        in_specs=[anyspace] * 3,
        out_specs=(anyspace,) * 3,
        scratch_shapes=[
            pltpu.VMEM((rows, hid), BF),
            pltpu.VMEM((2 * hid, hid), BF),
            pltpu.VMEM((nn, 8, hid), F32),
            pltpu.VMEM((2 * hid, hid), F32),
            pltpu.VMEM((1, hid), F32),
            dma((4,)), dma((4,)),
        ],
        name="hand_over",
    )(out, gw, gb)
    return out, gw, gb.reshape(hid)


def solution(mesh):
    nn, nf = mesh.shape["nodes"], mesh.shape["feat"]
    return jax.shard_map(
        functools.partial(per_device, nn, nf),
        mesh=mesh,
        in_specs=(
            P("feat", "nodes"),
            P(("nodes", "feat"), None),
            P(("nodes", "feat"), None, None, None),
            P(),
            P(),
            P(),
            P(),
            P(("nodes", "feat"), None),
        ),
        out_specs=(P(("nodes", "feat"), None), P(), P()),
        check_vma=False,
    )
```
